32 devices in a mesh: band: 4 (over y, x), grid: 8 (over z, core).
Axes of the slice: x: 2, y: 2, z: 4, core: 2. Of those that a mesh axis runs over, the one named last changes fastest.
Arguments:
- valence: bfloat16 [64, 96, 9216], P('band', 'grid'), may hold values from -6 to 6
- conduction: bfloat16 [32, 96, 9216], P('band', 'grid'), may hold values from -6 to 6
- screened: bfloat16 [6144, 6144], P('grid'), may hold values from -0.0007324219 to 0.0007324219
- blocks: int32 [2], replicated, may hold values from 0 to 7
- gsphere: int32 [6144], P('grid'), may hold values from 0 to 4095, as said below
Outputs:
- kernel: float32 [4, 64, 64], P('band', 'grid')
The draws below stay inside these ranges and needn't reach their ends.
Inputs may be any that keep to these rules, and one draw needn't show every extreme that they name: `gsphere`: distinct within each aligned block of 768 entries.
All inputs are finite; a program needn't handle non-finite values.
Results may differ from the reference program's by a relative error of at most 0.0093.
Values may be sent and summed in bfloat16 or wider, within the bound.
No kernel may reach another device: no remote copies, remote signals or barrier semaphores. Data moves between devices by JAX's collectives and lax.ppermute only.
A program may use at most 128 MiB of HBM per device.

```python
import math
import jax
import jax.numpy as jnp
from jax import lax

GRID_N = 96
KF = 32
NG = 6144
CB_DEV = 8
BLK = 8
CB = 32
NB = 8
NVAL = 64
NG_DEV = 768
N_BAND = 4
N_GRID = 8


def draw_gsphere(key, part):
    per_block = NG // N_GRID
    local_count = KF * KF * (KF // N_GRID)
    keys = jax.random.split(jax.random.fold_in(key, 17), N_GRID)

    def one_block(block_key):
        first_key, second_key = jax.random.split(block_key)
        inner = jax.random.permutation(first_key, local_count - 2)[:per_block - 2] + 1
        values = jnp.concatenate([jnp.array([0, local_count - 1], dtype=jnp.int32), inner.astype(jnp.int32)])
        return jax.random.permutation(second_key, values)
    return jax.vmap(one_block)(keys).reshape(NG).astype(jnp.int32)


def block_scale(own_key, shape, cuts, least, high):
    def one(axis_at, blocks):
        heights = jax.random.uniform(jax.random.fold_in(jax.random.fold_in(own_key, 6), axis_at), (blocks,), jnp.float32, least / len(cuts), high / len(cuts))
        return jnp.repeat(jnp.exp(heights), shape[axis_at] // blocks).reshape((-1,) + (1,) * (len(shape) - axis_at - 1))

    gain = one(*cuts[0])
    for cut in cuts[1:]:
        gain = gain * one(*cut)
    return gain


def gaussian(own_key, dims, scale, reach, pieces=(), held_as=jnp.bfloat16):
    factor_of = block_scale(own_key, dims, pieces, -0.22, 0.18) if pieces else 1.0
    values = jax.random.normal(own_key, dims, jnp.float32) * scale * factor_of
    return jnp.minimum(jnp.maximum(values, -reach), reach).astype(held_as)


def setup_inputs(seed: int = 0) -> dict:
    key_of = jax.random.split(jax.random.key(seed), 6)
    valence = gaussian(key_of[0], (NVAL, GRID_N, GRID_N * GRID_N), 1.0, 6.0, ((0, 4), (1, 8)))
    conduction = gaussian(key_of[1], (CB, GRID_N, GRID_N * GRID_N), 1.0, 6.0, ((0, 4), (1, 8)))
    screened = gaussian(key_of[2], (NG, NG), (2 * NG * NG) ** -0.5, 0.0007324219, ((0, 8),))
    blocks = jax.random.randint(key_of[3], (2,), 0, NB).astype(jnp.int32)
    gsphere = draw_gsphere(jax.random.fold_in(key_of[5], 71), 0)
    return {"valence": valence, "conduction": conduction, "screened": screened, "blocks": blocks, "gsphere": gsphere}


def fourier_parts(length, kept):
    positions = jnp.arange(length, dtype=jnp.int32)
    freqs = jnp.arange(kept, dtype=jnp.int32) - kept // 2
    phase = positions[:, None] * freqs[None, :] % length
    phases = phase.astype(jnp.float32) * (2.0 * math.pi / length)
    factor = 1.0 / math.sqrt(length)
    return (jnp.cos(phases) * factor, jnp.sin(phases) * factor)

def first_table(length, kept):
    cosine, sine = fourier_parts(length, kept)
    return jnp.stack([cosine, -sine], axis=2).astype(jnp.bfloat16)

def mixing_table(length, kept):
    cosine, sine = fourier_parts(length, kept)
    real_rows = jnp.stack([cosine, sine], axis=-1)
    imag_rows = jnp.stack([-sine, cosine], axis=-1)
    return jnp.stack([real_rows, imag_rows], axis=2).astype(jnp.bfloat16)

def reference(valence, conduction, screened, blocks, gsphere):
    z_table = first_table(GRID_N, KF).astype(jnp.float32)
    mixing = mixing_table(GRID_N, KF).astype(jnp.float32)
    high = lax.Precision.HIGHEST
    pick_a = lax.dynamic_slice_in_dim(valence, (blocks[0] * BLK).astype(jnp.int32), BLK, 0)
    pick_b = lax.dynamic_slice_in_dim(valence, (blocks[1] * BLK).astype(jnp.int32), BLK, 0)
    chosen = jnp.concatenate([pick_a, pick_b], axis=0)
    planes = KF // N_GRID
    number = jnp.arange(NG, dtype=jnp.int32)
    owner = number // NG_DEV
    freq_x = gsphere // (planes * KF)
    freq_y = owner * planes + gsphere // KF % planes
    freq_z = gsphere % KF
    index = ((freq_x * KF + freq_y) * KF + freq_z).astype(jnp.int32)
    cond_groups = conduction.reshape(N_BAND, CB_DEV, GRID_N, GRID_N * GRID_N)
    pairs = BLK * CB_DEV

    def per_band(cond):

        def per_valence(orbital):
            density = (orbital[None] * cond).reshape(CB_DEV, GRID_N, GRID_N, GRID_N)
            z_section = jnp.einsum('cxyz,zqi->cxyqi', density.astype(jnp.float32), z_table, precision=high).astype(jnp.bfloat16)
            y_section = jnp.einsum('cxyqi,ykoi->cxkqo', z_section.astype(jnp.float32), mixing, precision=high).astype(jnp.bfloat16)
            x_section = jnp.einsum('cxjqi,xkoi->ckjqo', y_section.astype(jnp.float32), mixing, precision=high).astype(jnp.bfloat16)
            flat = x_section.reshape(CB_DEV, KF * KF * KF, 2)
            return jnp.take(flat, index, axis=1)
        sphere = lax.map(per_valence, chosen)
        sphere = jnp.transpose(sphere, (2, 3, 0, 1)).reshape(NG, 2, 2 * pairs)
        side_a = sphere[:, :, :pairs]
        side_b = sphere[:, :, pairs:]
        screened_b = jnp.dot(screened, side_b.reshape(NG, 2 * pairs), preferred_element_type=jnp.float32)
        screened_b = screened_b.astype(jnp.bfloat16).reshape(NG, 2, pairs)
        return jnp.einsum('npi,npj->ij', side_a.astype(jnp.float32), screened_b.astype(jnp.float32), precision=high)
    return lax.map(per_band, cond_groups)
```

```python
import functools
import math

import jax
import jax.numpy as jnp
from jax import lax
from jax.experimental import pallas as pl
from jax.experimental.pallas import tpu as pltpu
from jax.sharding import PartitionSpec as P

GRID_N = 96
KF = 32
BLK = 8
XG = 4
LANES = XG * GRID_N
F32 = jnp.float32
BF16 = jnp.bfloat16


def fourier_parts(length, kept):
    positions = jnp.arange(length, dtype=jnp.int32)
    freqs = jnp.arange(kept, dtype=jnp.int32) - kept // 2
    phase = positions[:, None] * freqs[None, :] % length
    phases = phase.astype(F32) * (2.0 * math.pi / length)
    factor = 1.0 / math.sqrt(length)
    return (jnp.cos(phases) * factor).astype(BF16), (jnp.sin(phases) * factor).astype(BF16)


def y_table(cosine, sine):
    one = jnp.concatenate([cosine.T, -sine.T], axis=0)
    zero = jnp.zeros_like(one)
    return jnp.concatenate(
        [jnp.concatenate([one, zero], axis=1), jnp.concatenate([zero, one], axis=1)], axis=0
    )


def z_table(cosine, sine):
    from_real = jnp.stack([cosine, -sine], axis=1)
    from_imag = jnp.stack([sine, cosine], axis=1)
    both = jnp.stack([from_real, from_imag])
    same = jnp.eye(XG, dtype=BF16)
    table = same[None, :, None, :, None, None] * both[:, None, :, None, :, :]
    return table.reshape(2 * LANES, XG * 2 * KF)


def planes(orbitals):
    count, slab, _ = orbitals.shape
    groups = -(-slab // XG)
    orbitals = jnp.pad(orbitals, ((0, 0), (0, groups * XG - slab), (0, 0)))
    orbitals = orbitals.reshape(count, groups, XG, GRID_N, GRID_N)
    return jnp.transpose(orbitals, (0, 1, 3, 2, 4)).reshape(count, groups, GRID_N, LANES)


def front_kernel(here, val, cond, ytab, ztab, pick, wave, even, odd, mixed, section):
    conds, groups = cond.shape[0], cond.shape[1]
    cols = pick.shape[1]
    own_y = cols // KF
    for pair in range(conds // 2):
        for group in range(groups):
            orbital = val[0, group]
            density = jnp.concatenate(
                [orbital * cond[2 * pair, group], orbital * cond[2 * pair + 1, group]], axis=0
            )
            out = jnp.dot(ytab[...], density, preferred_element_type=F32).astype(BF16)
            for half in range(2):
                row = (2 * pair + half) * KF
                base = half * 2 * KF
                mixed[group, row:row + KF, :LANES] = out[base:base + KF]
                mixed[group, row:row + KF, LANES:] = out[base + KF:base + 2 * KF]
    for group in range(groups):
        value = jnp.dot(mixed[group], ztab[...], preferred_element_type=F32)
        section[2 * group] = value[:, :128]
        section[2 * group + 1] = value[:, 128:]

    def one_target(step, parity, out_ref):
        order = 2 * step + parity
        target = here[0] ^ order
        first = target * own_y
        parts = []
        for group in range(groups):
            for half in range(2):
                rows = [
                    section[2 * group + half, pl.ds(first + y, conds, stride=KF), :]
                    for y in range(own_y)
                ]
                for piece in range(4):
                    cut = slice(KF * piece, KF * piece + KF)
                    parts.append(jnp.concatenate([row[:, cut] for row in rows], axis=1))
        left = jnp.concatenate(parts, axis=0).astype(BF16)
        found = jnp.dot(left, pick[order], preferred_element_type=F32)
        real = imag = None
        count = XG * groups
        for x in range(count):
            cosine = wave[order, x:x + 1, :]
            sine = wave[order, count + x:count + x + 1, :]
            re = found[2 * x * conds:(2 * x + 1) * conds]
            im = found[(2 * x + 1) * conds:(2 * x + 2) * conds]
            add_real = re * cosine + im * sine
            add_imag = im * cosine - re * sine
            real = add_real if real is None else real + add_real
            imag = add_imag if imag is None else imag + add_imag
        out_ref[step] = jnp.concatenate([real, imag], axis=0).astype(BF16)

    def body(step, carry):
        one_target(step, 0, even)
        one_target(step, 1, odd)
        return carry

    lax.fori_loop(0, even.shape[0], body, 0)


def front(here, vals, cond, ytab, ztab, pick, wave):
    count, groups = vals.shape[:2]
    conds = cond.shape[0]
    targets, cols, own = pick.shape
    rows = 2 * conds
    shape = jax.ShapeDtypeStruct((targets // 2, count * rows, own), BF16)
    whole = lambda a: pl.BlockSpec(a.shape, lambda v, h: (0,) * a.ndim)
    spec = pltpu.PrefetchScalarGridSpec(
        num_scalar_prefetch=1,
        grid=(count,),
        in_specs=[
            pl.BlockSpec((1,) + vals.shape[1:], lambda v, h: (v, 0, 0, 0)),
            whole(cond), whole(ytab), whole(ztab), whole(pick), whole(wave),
        ],
        out_specs=[pl.BlockSpec((targets // 2, rows, own), lambda v, h: (0, v, 0))] * 2,
        scratch_shapes=[
            pltpu.VMEM((groups, conds * KF, 2 * LANES), BF16),
            pltpu.VMEM((2 * groups, conds * KF, XG * KF), F32),
        ],
    )
    return pl.pallas_call(
        front_kernel,
        grid_spec=spec,
        out_shape=[shape, shape],
        compiler_params=pltpu.CompilerParams(vmem_limit_bytes=48 * 1024 * 1024),
        cost_estimate=pl.CostEstimate(flops=count * 900_000_000, bytes_accessed=count * 2_000_000, transcendentals=0),
        name="front",
    )(here, vals, cond, ytab, ztab, pick, wave)


def screen_kernel(here, *refs):
    *pieces, w_even, w_odd, even, odd, side = refs

    @pl.when(pl.program_id(0) == 0)
    def _():
        total = pieces[0][...].astype(F32)
        for piece in pieces[1:]:
            total = total + piece[...].astype(F32)
        side[...] = total.astype(BF16)

    even[0] = jnp.dot(side[...], w_even[...], preferred_element_type=F32).astype(BF16)
    odd[0] = jnp.dot(side[...], w_odd[...], preferred_element_type=F32).astype(BF16)


def screen(here, pieces, screened, targets):
    rows, own = pieces[0].shape
    if own % 128:
        side = sum(p.astype(F32) for p in pieces).astype(BF16)
        part = jnp.dot(side, screened, preferred_element_type=F32).astype(BF16)
        part = jnp.transpose(part.reshape(rows, targets, own), (1, 0, 2))
        part = jnp.take(part, here[0] ^ jnp.arange(targets), axis=0)
        return part[0::2], part[1::2]
    shape = jax.ShapeDtypeStruct((targets // 2, rows, own), BF16)
    spec = pltpu.PrefetchScalarGridSpec(
        num_scalar_prefetch=1,
        grid=(targets // 2,),
        in_specs=[pl.BlockSpec((rows, own), lambda r, h: (0, 0))] * len(pieces) + [
            pl.BlockSpec((own, own), lambda r, h: (0, h[0] ^ (2 * r))),
            pl.BlockSpec((own, own), lambda r, h: (0, h[0] ^ (2 * r + 1))),
        ],
        out_specs=[pl.BlockSpec((1, rows, own), lambda r, h: (r, 0, 0))] * 2,
        scratch_shapes=[pltpu.VMEM((rows, own), BF16)],
    )
    return pl.pallas_call(
        screen_kernel,
        grid_spec=spec,
        out_shape=[shape, shape],
        compiler_params=pltpu.CompilerParams(vmem_limit_bytes=32 * 1024 * 1024),
        cost_estimate=pl.CostEstimate(flops=2 * rows * own * own * targets, bytes_accessed=2 * own * own * targets, transcendentals=0),
        name="screen",
    )(here, *pieces, screened, screened)


def close_kernel(count, first, *refs):
    ins, out = refs[:-1], refs[-1]
    sides = []
    for group in (ins[:count], ins[count:]):
        total = group[0][...].astype(F32)
        for piece in group[1:]:
            total = total + piece[...].astype(F32)
        rows, own = total.shape
        total = total.reshape(rows // (2 * first), 2, first, own)
        sides.append([total[:, part].reshape(rows // 2, own).astype(BF16) for part in range(2)])
    product = None
    for left, right in zip(*sides, strict=True):
        term = lax.dot_general(left, right, (((1,), (1,)), ((), ())), preferred_element_type=F32)
        product = term if product is None else product + term
    out[...] = product


def close(u_pieces, b_pieces, conds):
    rows = u_pieces[0].shape[0] // 2
    return pl.pallas_call(
        functools.partial(close_kernel, len(u_pieces), conds),
        out_shape=jax.ShapeDtypeStruct((rows, rows), F32),
        name="close",
    )(*u_pieces, *b_pieces)


def swap(array, axis, mask, size):
    return lax.ppermute(array, axis, [(i, i ^ mask) for i in range(size)])


def gather_sums(even, odd, targets):
    total = (even.astype(F32) + swap(odd, "grid", 1, targets).astype(F32)).astype(even.dtype)
    return [total[0]] + [swap(total[r], "grid", 2 * r, targets) for r in range(1, targets // 2)]


def ring_order(size):
    return [0, 1, 3, 2] if size == 4 else list(range(size))


def round_ring(own, holder, size, reverse):
    order = ring_order(size)
    if reverse:
        order = order[::-1]
    pairs = [(order[i], order[(i + 1) % size]) for i in range(size)]
    place = [0] * size
    for i, device in enumerate(order):
        place[device] = i
    place = jnp.array(place, jnp.int32)
    away = (place[lax.axis_index("band")] - place[holder]) % size
    chunks = len(own)
    got = []
    for step in range(chunks + size - 2):
        mine = own[min(step, chunks - 1)]
        sent = mine if step == 0 else jnp.where(away == 0, mine, got[-1])
        got.append(lax.ppermute(sent, "band", pairs))
    out = []
    for j in range(chunks):
        value = own[j]
        for hop in range(1, size):
            value = jnp.where(away == hop, got[j + hop - 1], value)
        out.append(value)
    return out


def per_device(sizes, valence, conduction, screened, blocks, gsphere):
    n_band, n_grid = sizes
    held = valence.shape[0] // BLK
    conds, slab = conduction.shape[:2]
    cols = KF // n_grid * KF
    here = lax.axis_index("grid").astype(jnp.int32)
    at = here[None]

    cosine, sine = fourier_parts(GRID_N, KF)
    ytab, ztab = y_table(cosine, sine), z_table(cosine, sine)
    targets = here ^ jnp.arange(n_grid, dtype=jnp.int32)
    points = jnp.take(lax.all_gather(gsphere, "grid", axis=0), targets, axis=0)
    pick = (jnp.arange(cols, dtype=jnp.int32)[None, :, None] == (points % cols)[:, None, :]).astype(BF16)
    turn = (jnp.arange(KF, dtype=jnp.int32)[None, :, None] == (points // cols)[:, None, :]).astype(BF16)
    fill = -slab % XG
    local = lambda t: jnp.pad(lax.dynamic_slice_in_dim(t, here * slab, slab, 0), ((0, fill), (0, 0)))
    phase = jnp.concatenate([local(cosine), local(sine)], axis=0)
    wave = jnp.einsum("xq,rqn->rxn", phase, turn, preferred_element_type=F32)

    cond = planes(conduction)

    def chosen(block):
        mine = planes(lax.dynamic_slice_in_dim(valence, block % held * BLK, BLK, 0))
        holder = block // held
        half = BLK // 2
        right = round_ring([mine[j] for j in range(half)], holder, n_band, False)
        left = round_ring([mine[j] for j in range(half, BLK)], holder, n_band, True)
        return jnp.stack(right + left)

    side_a = gather_sums(*front(at, chosen(blocks[0]), cond, ytab, ztab, pick, wave), n_grid)
    part_b = front(at, chosen(blocks[1]), cond, ytab, ztab, pick, wave)
    part_u = screen(at, side_a, screened, n_grid)
    side_b = gather_sums(*part_b, n_grid)
    side_u = gather_sums(*part_u, n_grid)
    share = close(side_u, side_b, conds)
    share = jnp.take(share.reshape(n_grid, -1, share.shape[1]), targets, axis=0)
    pieces = gather_sums(share[0::2], share[1::2], n_grid)
    return sum(pieces)[None]


def solution(mesh):
    sizes = (mesh.shape["band"], mesh.shape["grid"])
    in_specs = (P("band", "grid", None), P("band", "grid", None), P("grid", None), P(), P("grid"))
    out_specs = P("band", "grid", None)
    return jax.shard_map(
        functools.partial(per_device, sizes), mesh=mesh, in_specs=in_specs, out_specs=out_specs, check_vma=False
    )
```

```python
import functools
import math

import jax
import jax.numpy as jnp
import numpy as np
from jax import lax
from jax.experimental import pallas as pl
from jax.experimental.pallas import tpu as pltpu
from jax.sharding import PartitionSpec as P

GRID_N = 96
KF = 32
BLK = 8
XG = 4
LANES = XG * GRID_N
F32 = jnp.float32
BF16 = jnp.bfloat16


def fourier_parts(length, kept):
    phase = np.arange(length)[:, None] * (np.arange(kept) - kept // 2)[None, :] % length * (2.0 * math.pi / length)
    return (np.cos(phase) / math.sqrt(length)).astype(BF16), (np.sin(phase) / math.sqrt(length)).astype(BF16)


def y_table(cosine, sine):
    order = np.arange(GRID_N).reshape(-1, XG).T.reshape(-1)
    one = np.concatenate([cosine[order].T, -sine[order].T], axis=0)
    zero = np.zeros_like(one)
    return np.concatenate([np.concatenate([one, zero], axis=1), np.concatenate([zero, one], axis=1)], axis=0)


def z_table(cosine, sine):
    both = np.stack([np.stack([cosine, -sine], axis=1), np.stack([sine, cosine], axis=1)])
    table = np.zeros((2, XG, GRID_N, XG, 2, KF), BF16)
    for x in range(XG):
        table[:, x, :, x] = both
    return table.reshape(2 * LANES, XG * 2 * KF)


def x_phases(cosine, sine, n_grid):
    slab = GRID_N // n_grid
    fill = ((0, 0), (0, -slab % XG), (0, 0))
    parts = [np.pad(t.reshape(n_grid, slab, KF).astype(np.float32), fill) for t in (cosine, sine)]
    return np.concatenate(parts, axis=1).astype(BF16)


HOLDS = np.array([[0, 1, 3, 2], [0, 2, 3, 1], [1, 3, 0, 2], [1, 0, 3, 2]])
SOURCES = np.array([[0, 1, 1, 0], [2, 4, 2, 3], [3, 5, 2, 3], [4, 5, 2, 3]])


def slots_of():
    quarter = BLK // 4
    return np.argsort((quarter * HOLDS[:, :, None] + np.arange(quarter)).reshape(4, BLK), axis=1)


def planes_kernel(outs_of, blocks, src, *refs):
    outs, rows = refs[:-1], refs[-1]
    orbital = src[0]
    slab = orbital.shape[0]
    step = -(-slab // 8) * 8
    high = GRID_N // XG
    for y in range(high):
        for t in range(LANES // 128):
            cut = slice(y * LANES + 128 * t, y * LANES + 128 * t + 128)
            rows[t, y * step:y * step + slab, :] = orbital[:, cut].astype(F32)

    def write(out):
        for group in range(out.shape[1]):
            wide = []
            for x in range(XG * group, XG * group + XG):
                if x < slab:
                    wide.append(jnp.concatenate([rows[t, pl.ds(x, high, stride=step), :] for t in range(LANES // 128)], axis=1))
                else:
                    wide.append(jnp.zeros((high, LANES), F32))
            lines = [
                jnp.concatenate([w[:, GRID_N * low:GRID_N * low + GRID_N] for w in wide], axis=1) for low in range(XG)
            ]
            out[0, group] = jnp.concatenate(lines, axis=0).astype(BF16)

    if len(outs) == 1:
        write(outs[0])
        return
    for i, out in enumerate(outs):
        @pl.when(pl.program_id(0) // outs_of == i)
        def _(out=out):
            write(out)


def planes(orbitals, blocks, first, count, outs):
    slab, size = orbitals.shape[1:]
    groups = -(-slab // XG)
    each = count // outs
    spec = pltpu.PrefetchScalarGridSpec(
        num_scalar_prefetch=1,
        grid=(count,),
        in_specs=[pl.BlockSpec((1, slab, size), lambda f, b: (first(b) + f, 0, 0))],
        out_specs=[
            pl.BlockSpec((1, groups, GRID_N, LANES), lambda f, b, i=i: (jnp.clip(f - i * each, 0, each - 1), 0, 0, 0))
            for i in range(outs)
        ],
        scratch_shapes=[pltpu.VMEM((LANES // 128, GRID_N // XG * (-(-slab // 8) * 8), 128), F32)],
    )
    return pl.pallas_call(
        functools.partial(planes_kernel, each),
        grid_spec=spec,
        out_shape=[jax.ShapeDtypeStruct((each, groups, GRID_N, LANES), BF16)] * outs,
        compiler_params=pltpu.CompilerParams(vmem_limit_bytes=16 * 1024 * 1024),
        cost_estimate=pl.CostEstimate(flops=0, bytes_accessed=4 * count * slab * size, transcendentals=0),
        name="planes",
    )(blocks, orbitals)


def tables_kernel(*refs):
    *points, phases, pick, wave = refs
    cols = pick.shape[1]
    phase = phases[lax.axis_index("grid")]
    for r in range(pick.shape[0]):
        point = points[r // 2][r % 2:r % 2 + 1, :]
        shape = (cols, point.shape[1])
        found = lax.broadcasted_iota(jnp.int32, shape, 0) == jnp.broadcast_to(point & (cols - 1), shape)
        pick[r] = found.astype(F32).astype(BF16)
        shape = (KF, point.shape[1])
        turn = lax.broadcasted_iota(jnp.int32, shape, 0) == jnp.broadcast_to(point >> (cols.bit_length() - 1), shape)
        wave[r] = jnp.dot(phase, turn.astype(F32).astype(BF16), preferred_element_type=F32)


def tables(points, phases, cols):
    targets, own = 2 * len(points), points[0].shape[1]
    return pl.pallas_call(
        tables_kernel,
        out_shape=[
            jax.ShapeDtypeStruct((targets, cols, own), BF16),
            jax.ShapeDtypeStruct((targets, phases.shape[1], own), F32),
        ],
        compiler_params=pltpu.CompilerParams(vmem_limit_bytes=16 * 1024 * 1024),
        cost_estimate=pl.CostEstimate(flops=0, bytes_accessed=3 * targets * cols * own, transcendentals=0),
        name="tables",
    )(*points, phases)


def front_kernel(sources, find, blocks, source_of, *refs):
    parts_in, refs = refs[:sources], refs[sources:]
    cond, ytab, ztab, pick, wave, even, odd, vals, mixed, section, arrived = refs
    conds, groups = cond.shape[0], cond.shape[1]
    cols = pick.shape[1]
    own_y = cols // KF
    count = vals.shape[0]
    now = pl.program_id(0)

    @pl.when(now == 0)
    def _():
        for f in range(count):
            wanted, inside = find(blocks, source_of, f)
            for s in range(sources):
                @pl.when(wanted == s)
                def _(f=f, s=s):
                    pltpu.make_async_copy(parts_in[s].at[inside], vals.at[f], arrived.at[f]).start()

    pltpu.make_async_copy(parts_in[0].at[0], vals.at[now], arrived.at[now]).wait()
    for pair in range(conds // 2):
        for group in range(groups):
            orbital = vals[now, group]
            density = jnp.concatenate(
                [orbital * cond[2 * pair, group], orbital * cond[2 * pair + 1, group]], axis=0
            )
            out = jnp.dot(ytab[...], density, preferred_element_type=F32).astype(BF16)
            for half in range(2):
                row = (2 * pair + half) * KF
                base = half * 2 * KF
                mixed[group, row:row + KF, :LANES] = out[base:base + KF]
                mixed[group, row:row + KF, LANES:] = out[base + KF:base + 2 * KF]
    for group in range(groups):
        value = jnp.dot(mixed[group], ztab[...], preferred_element_type=F32)
        section[2 * group] = value[:, :128]
        section[2 * group + 1] = value[:, 128:]

    def one_target(step, parity, out_ref):
        order = 2 * step + parity
        target = lax.axis_index("grid").astype(jnp.int32) ^ order
        first = target * own_y
        parts = []
        for group in range(groups):
            for half in range(2):
                rows = [
                    section[2 * group + half, pl.ds(first + y, conds, stride=KF), :]
                    for y in range(own_y)
                ]
                for piece in range(4):
                    cut = slice(KF * piece, KF * piece + KF)
                    parts.append(jnp.concatenate([row[:, cut] for row in rows], axis=1))
        left = jnp.concatenate(parts, axis=0).astype(BF16)
        found = jnp.dot(left, pick[order], preferred_element_type=F32)
        real = imag = None
        count = XG * groups
        for x in range(count):
            cosine = wave[order, x:x + 1, :]
            sine = wave[order, count + x:count + x + 1, :]
            re = found[2 * x * conds:(2 * x + 1) * conds]
            im = found[(2 * x + 1) * conds:(2 * x + 2) * conds]
            add_real = re * cosine + im * sine
            add_imag = im * cosine - re * sine
            real = add_real if real is None else real + add_real
            imag = add_imag if imag is None else imag + add_imag
        out_ref[step] = jnp.concatenate([real, imag], axis=0).astype(BF16)

    def body(step, carry):
        one_target(step, 0, even)
        one_target(step, 1, odd)
        return carry

    lax.fori_loop(0, even.shape[0], body, 0)


def front(find, count, blocks, sources, cond, ytab, ztab, pick, wave):
    conds, groups = cond.shape[:2]
    targets, cols, own = pick.shape
    rows = 2 * conds
    shape = jax.ShapeDtypeStruct((targets // 2, count * rows, own), BF16)
    whole = lambda a: pl.BlockSpec(a.shape, lambda v, b, t: (0,) * a.ndim)
    spec = pltpu.PrefetchScalarGridSpec(
        num_scalar_prefetch=2,
        grid=(count,),
        in_specs=[pl.BlockSpec(memory_space=pl.ANY)] * len(sources) + [
            whole(cond), whole(ytab), whole(ztab), whole(pick), whole(wave),
        ],
        out_specs=[pl.BlockSpec((targets // 2, rows, own), lambda v, b, t: (0, v, 0))] * 2,
        scratch_shapes=[
            pltpu.VMEM((count,) + cond.shape[1:], BF16),
            pltpu.VMEM((groups, conds * KF, 2 * LANES), BF16),
            pltpu.VMEM((2 * groups, conds * KF, XG * KF), F32),
            pltpu.SemaphoreType.DMA((count,)),
        ],
    )
    return pl.pallas_call(
        functools.partial(front_kernel, len(sources), find),
        grid_spec=spec,
        out_shape=[shape, shape],
        compiler_params=pltpu.CompilerParams(vmem_limit_bytes=40 * 1024 * 1024),
        cost_estimate=pl.CostEstimate(flops=count * 900_000_000, bytes_accessed=count * 2_000_000, transcendentals=0),
        name="front",
    )(blocks, jnp.asarray(SOURCES.reshape(-1), jnp.int32), *sources, cond, ytab, ztab, pick, wave)


def screen_kernel(here, *refs):
    *pieces, w_even, w_odd, even, odd, side = refs

    @pl.when(pl.program_id(0) == 0)
    def _():
        total = pieces[0][...].astype(F32)
        for piece in pieces[1:]:
            total = total + piece[...].astype(F32)
        side[...] = total.astype(BF16)

    even[0] = jnp.dot(side[...], w_even[...], preferred_element_type=F32).astype(BF16)
    odd[0] = jnp.dot(side[...], w_odd[...], preferred_element_type=F32).astype(BF16)


def screen(here, pieces, screened, targets):
    rows, own = pieces[0].shape
    if own % 128:
        side = sum(p.astype(F32) for p in pieces).astype(BF16)
        part = jnp.dot(side, screened, preferred_element_type=F32).astype(BF16)
        part = jnp.transpose(part.reshape(rows, targets, own), (1, 0, 2))
        part = jnp.take(part, here[0] ^ jnp.arange(targets), axis=0)
        return part[0::2], part[1::2]
    shape = jax.ShapeDtypeStruct((targets // 2, rows, own), BF16)
    spec = pltpu.PrefetchScalarGridSpec(
        num_scalar_prefetch=1,
        grid=(targets // 2,),
        in_specs=[pl.BlockSpec((rows, own), lambda r, h: (0, 0))] * len(pieces) + [
            pl.BlockSpec((own, own), lambda r, h: (0, h[0] ^ (2 * r))),
            pl.BlockSpec((own, own), lambda r, h: (0, h[0] ^ (2 * r + 1))),
        ],
        out_specs=[pl.BlockSpec((1, rows, own), lambda r, h: (r, 0, 0))] * 2,
        scratch_shapes=[pltpu.VMEM((rows, own), BF16)],
    )
    return pl.pallas_call(
        screen_kernel,
        grid_spec=spec,
        out_shape=[shape, shape],
        compiler_params=pltpu.CompilerParams(vmem_limit_bytes=32 * 1024 * 1024),
        cost_estimate=pl.CostEstimate(flops=2 * rows * own * own * targets, bytes_accessed=2 * own * own * targets, transcendentals=0),
        name="screen",
    )(here, *pieces, screened, screened)


def close_kernel(split, place, blocks, slot_of, *refs):
    ins, outs, sums = refs[:sum(map(sum, split))], refs[sum(map(sum, split)):-2], refs[-2:]
    sides = []
    for side, pieces in enumerate(split):
        first = 0
        for count in pieces:
            group, ins = ins[:count], ins[count:]
            total = group[0][...].astype(F32)
            for piece in group[1:]:
                total = total + piece[...].astype(F32)
            rows, own = total.shape
            unit = sums[side].shape[1]
            sums[side][first:first + rows // unit] = total.reshape(rows // unit, unit, own)
            first += rows // unit
        units = [sums[side][place(blocks, slot_of, side, f)] for f in range(first)]
        half = unit // 2
        sides.append([
            jnp.concatenate([u[half * part:half * part + half] for u in units], axis=0).astype(BF16) for part in range(2)
        ])
    product = None
    for left, right in zip(*sides, strict=True):
        term = lax.dot_general(left, right, (((1,), (1,)), ((), ())), preferred_element_type=F32)
        product = term if product is None else product + term
    if len(outs) == 1:
        outs[0][...] = product
    else:
        rows = outs[0].shape[1]
        for r in range(product.shape[0] // rows):
            outs[r % 2][r // 2] = product[r * rows:(r + 1) * rows]


def close(place, blocks, u_pieces, b_pieces, conds, targets, by_target):
    split = [[len(p) for p in side] for side in (u_pieces, b_pieces)]
    flat = [x for side in (u_pieces, b_pieces) for p in side for x in p]
    functions = BLK
    rows = functions * conds
    own = flat[0].shape[1]
    if by_target:
        out = [jax.ShapeDtypeStruct((targets // 2, rows // targets, rows), F32)] * 2
    else:
        out = [jax.ShapeDtypeStruct((rows, rows), F32)]
    spec = pltpu.PrefetchScalarGridSpec(
        num_scalar_prefetch=2,
        grid=(1,),
        in_specs=[pl.BlockSpec(x.shape, lambda i, b, t: (0, 0)) for x in flat],
        out_specs=[pl.BlockSpec(o.shape, lambda i, b, t, o=o: (0,) * len(o.shape)) for o in out],
        scratch_shapes=[pltpu.VMEM((functions, 2 * conds, own), F32)] * 2,
    )
    return pl.pallas_call(
        functools.partial(close_kernel, split, place),
        grid_spec=spec,
        out_shape=out,
        cost_estimate=pl.CostEstimate(flops=4 * rows * rows * own, bytes_accessed=8 * rows * own, transcendentals=0),
        compiler_params=pltpu.CompilerParams(vmem_limit_bytes=32 * 1024 * 1024),
        name="close",
    )(blocks, jnp.asarray(slots_of().reshape(-1), jnp.int32), *flat)


def swap(array, axis, mask, size):
    return lax.ppermute(array, axis, [(i, i ^ mask) for i in range(size)])


def gather_sums(even, odd, targets):
    total = (even.astype(F32) + swap(odd, "grid", 1, targets).astype(F32)).astype(even.dtype)
    return [total[0]] + [swap(total[r], "grid", 2 * r, targets) for r in range(1, targets // 2)]


def round_ring(own, holder, size, reverse):
    order = list(range(size))
    if reverse:
        order = order[::-1]
    pairs = [(order[i], order[(i + 1) % size]) for i in range(size)]
    place = [0] * size
    for i, device in enumerate(order):
        place[device] = i
    place = jnp.array(place, jnp.int32)
    away = (place[lax.axis_index("band")] - place[holder]) % size
    chunks = len(own)
    got = []
    for step in range(chunks + size - 2):
        mine = own[min(step, chunks - 1)]
        sent = mine if step == 0 else jnp.where(away == 0, mine, got[-1])
        got.append(lax.ppermute(sent, "band", pairs))
    out = []
    for j in range(chunks):
        value = own[j]
        for hop in range(1, size):
            value = jnp.where(away == hop, got[j + hop - 1], value)
        out.append(value)
    return out


def by_ring(valence, blocks, side, held, size):
    half = BLK // 2
    own = planes(valence, blocks, lambda b: b[side] % held * BLK, BLK, BLK)
    right = round_ring(own[:half], blocks[side] // held, size, False)
    left = round_ring(own[half:], blocks[side] // held, size, True)
    return right, left


def by_swaps(early, valence, blocks, side, held):
    owner = lax.axis_index("band") == blocks[side] // held
    across = lambda a: swap(a, "band", 1, 4)
    along = lambda a: swap(a, "band", 2, 4)
    own0, own1 = early
    own2, own3 = planes(valence, blocks, lambda b: b[side] % held * BLK + BLK // 2, BLK // 2, 2)
    x1, y1 = across(own0), along(own1)
    x2 = across(jnp.where(owner, own2, y1))
    y2 = along(jnp.where(owner, own3, x1))
    x3 = across(jnp.where(owner, own3, y2))
    y3 = along(jnp.where(owner, own2, x2))
    return [own0, own1, x1, y1, x2, y2], [own2, own3, x3, y3]


def per_device(sizes, valence, conduction, screened, blocks, gsphere):
    n_band, n_grid = sizes
    held = valence.shape[0] // BLK
    conds, own = conduction.shape[0], gsphere.shape[0]
    cols = KF // n_grid * KF
    half, quarter = BLK // 2, BLK // 4
    swaps = n_band == 4
    at = lax.axis_index("grid").astype(jnp.int32)[None]
    cosine, sine = fourier_parts(GRID_N, KF)
    ytab, ztab = jnp.asarray(y_table(cosine, sine)), jnp.asarray(z_table(cosine, sine))

    def role(b, side):
        return lax.axis_index("band").astype(jnp.int32) ^ (b[side] // held)

    if swaps:
        early = [planes(valence, blocks, lambda b, s=s: b[s] % held * BLK, half, 2) for s in range(2)]
        chosen = [by_swaps(early[s], valence, blocks, s, held) for s in range(2)]
    else:
        chosen = [by_ring(valence, blocks, s, held, n_band) for s in range(2)]
    cond, = planes(conduction, blocks, lambda b: 0, conds, 1)

    pair = gsphere.reshape(1, own)
    pair = jnp.concatenate([pair, swap(pair, "grid", 1, n_grid)], axis=0)
    points = [pair] + [swap(pair, "grid", 2 * r, n_grid) for r in range(1, n_grid // 2)]
    pick, wave = tables(points, jnp.asarray(x_phases(cosine, sine, n_grid)), cols)

    def part(side, late):
        def find(b, source_of, f):
            if not swaps:
                return f, 0
            return source_of[role(b, side) * 4 + 2 * late + f // quarter], f % quarter
        return front(find, half, blocks, chosen[side][late], cond, ytab, ztab, pick, wave)

    part_a, part_b = [], []
    for late in range(2):
        part_a.append(part(0, late))
        part_b.append(part(1, late))
    side_a = [gather_sums(*p, n_grid) for p in part_a]
    side_u = [gather_sums(*screen(at, p, screened, n_grid), n_grid) for p in side_a]
    side_b = [gather_sums(*p, n_grid) for p in part_b]

    by_target = n_grid == BLK

    def place(b, slot_of, side, f):
        if side == 0 and by_target:
            f = f ^ lax.axis_index("grid").astype(jnp.int32)
        return slot_of[role(b, side) * BLK + f] if swaps else f

    shares = close(place, blocks, side_u, side_b, conds, n_grid, by_target)
    if not by_target:
        share = shares[0].reshape(n_grid, -1, shares[0].shape[1])
        share = jnp.take(share, at ^ jnp.arange(n_grid, dtype=jnp.int32), axis=0)
        shares = share[0::2], share[1::2]
    return sum(gather_sums(*shares, n_grid))[None]


def solution(mesh):
    sizes = (mesh.shape["band"], mesh.shape["grid"])
    in_specs = (P("band", "grid", None), P("band", "grid", None), P("grid", None), P(), P("grid"))
    out_specs = P("band", "grid", None)
    return jax.shard_map(
        functools.partial(per_device, sizes), mesh=mesh, in_specs=in_specs, out_specs=out_specs, check_vma=False
    )
```

```python
import functools
import math

import jax
import jax.numpy as jnp
import numpy as np
from jax import lax
from jax.experimental import pallas as pl
from jax.experimental.pallas import tpu as pltpu
from jax.sharding import PartitionSpec as P

GRID_N = 96
KF = 32
BLK = 8
XG = 4
LANES = XG * GRID_N
F32 = jnp.float32
BF16 = jnp.bfloat16
WHOLE_VMEM = 56 * 1024 * 1024
PART_VMEM = 20 * 1024 * 1024
FRONT_VMEM = 24 * 1024 * 1024


def fourier_parts(length, kept):
    phase = np.arange(length)[:, None] * (np.arange(kept) - kept // 2)[None, :] % length * (2.0 * math.pi / length)
    return (np.cos(phase) / math.sqrt(length)).astype(BF16), (np.sin(phase) / math.sqrt(length)).astype(BF16)


def classes_of(own_y):
    return XG if own_y == XG else 1


def y_table(cosine, sine, classes):
    order = np.arange(GRID_N).reshape(-1, XG).T.reshape(-1)
    one = np.stack([cosine[order].T, -sine[order].T]).reshape(2, KF // classes, classes, GRID_N)
    table = np.zeros((2, classes, 2, KF // classes, 2, GRID_N), BF16)
    for pair in range(2):
        table[:, :, pair, :, pair] = one.transpose(0, 2, 1, 3)
    return table.reshape(4 * KF, 2 * GRID_N)


def z_table(cosine, sine, classes):
    both = np.stack([np.stack([cosine, -sine], axis=1), np.stack([sine, cosine], axis=1)])
    table = np.zeros((2, XG, GRID_N, XG, 2, KF), BF16)
    for x in range(XG):
        table[:, x, :, x] = both
    table = table.reshape(2 * LANES, 2, 4, KF)
    return np.stack([np.roll(table, i, axis=2).reshape(2 * LANES, XG * 2 * KF) for i in range(classes)])


def x_phases(n_grid):
    slab = GRID_N // n_grid
    lines = -(-slab // XG) * XG // 2
    freqs = 2.0 * math.pi / GRID_N * (np.arange(KF) - KF // 2)
    away = (lines - 0.5 - np.arange(lines))[:, None] * freqs
    middle = (slab * np.arange(n_grid) + lines - 0.5)[:, None, None] * freqs
    scale = 1.0 / math.sqrt(GRID_N)
    fixed = np.broadcast_to(np.concatenate([np.cos(away), np.sin(away)]), (n_grid, 2 * lines, KF))
    rows = np.concatenate([fixed, np.cos(middle) * scale, np.sin(middle) * scale], axis=1)
    rows = np.pad(rows, ((0, 0), (0, -rows.shape[1] % 8), (0, 0)))
    high = rows.astype(BF16)
    return np.stack([high, (rows - high.astype(np.float64)).astype(BF16)], axis=1)


HOLDS = np.array([[0, 1, 3, 2], [0, 2, 3, 1], [1, 3, 0, 2], [1, 0, 3, 2]])
SOURCES = np.array([[0, 1, 1, 0], [2, 4, 2, 3], [3, 5, 2, 3], [4, 5, 2, 3]])


def slots_of():
    quarter = BLK // 4
    return np.argsort((quarter * HOLDS[:, :, None] + np.arange(quarter)).reshape(4, BLK), axis=1)


def planes_kernel(firsts, blocks, src, *refs):
    outs, (rows, held, arrived) = refs[:-3], refs[-3:]
    groups, together = outs[0].shape[1], held.shape[0] // outs[0].shape[1]
    functions = src.shape[1]
    tiles, high = LANES // 128, GRID_N // XG

    def fetch(group):
        part = pl.ds(together * group, together)
        return pltpu.make_async_copy(src.at[part], held.at[part], arrived.at[group])

    for group in range(groups):
        fetch(group).start()
    for group in range(groups):
        fetch(group).wait()
        for x in range(together):
            for y in range(high):
                for t in range(tiles):
                    cut = slice(y * LANES + 128 * t, y * LANES + 128 * t + 128)
                    rows[x * tiles + t, y * functions:(y + 1) * functions, :] = held[together * group + x, :, cut].astype(F32)
        for first, out in zip(firsts, outs, strict=True):
            for f in range(out.shape[0]):
                at = pl.ds(first(blocks) + f, high, stride=functions)
                wide = [jnp.concatenate([rows[x * tiles + t, at, :] for t in range(tiles)], axis=1) for x in range(together)]
                wide += [jnp.zeros((high, LANES), F32)] * (XG - together)
                lines = [
                    jnp.concatenate([w[:, GRID_N * low:GRID_N * low + GRID_N] for w in wide], axis=1) for low in range(XG)
                ]
                out[f, group] = jnp.concatenate(lines, axis=0).astype(BF16)


def planes(orbitals, blocks, firsts, count, stay=False):
    orbitals = jnp.transpose(orbitals, (1, 0, 2))
    slab, functions, size = orbitals.shape
    together = min(XG, slab)
    groups = slab // together
    shape = (count, groups, GRID_N, LANES)
    spec = pltpu.PrefetchScalarGridSpec(
        num_scalar_prefetch=1,
        grid=(1,),
        in_specs=[pl.BlockSpec(memory_space=pl.ANY)],
        out_specs=[pl.BlockSpec(shape, lambda g, b: (0, 0, 0, 0))] * len(firsts),
        scratch_shapes=[
            pltpu.VMEM((LANES // 128 * together, GRID_N // XG * functions, 128), F32),
            pltpu.VMEM((slab, functions, size), BF16),
            pltpu.SemaphoreType.DMA((groups,)),
        ],
    )
    return pl.pallas_call(
        functools.partial(planes_kernel, firsts),
        grid_spec=spec,
        out_shape=[jax.ShapeDtypeStruct(shape, BF16)] * len(firsts),
        compiler_params=pltpu.CompilerParams(vmem_limit_bytes=WHOLE_VMEM if stay else PART_VMEM),
        cost_estimate=pl.CostEstimate(flops=0, bytes_accessed=4 * slab * functions * size, transcendentals=0),
        name="planes",
    )(blocks, orbitals)


def tables_kernel(*refs):
    *points, phases, pick, wave = refs
    cols = pick.shape[1]
    phase = phases[lax.axis_index("grid")]
    for r in range(pick.shape[0]):
        half = points[0].shape[0]
        point = points[r // half][r % half:r % half + 1, :]
        shape = (cols, point.shape[1])
        found = lax.broadcasted_iota(jnp.int32, shape, 0) == jnp.broadcast_to(point & (cols - 1), shape)
        pick[r] = found.astype(F32).astype(BF16)
        shape = (KF, point.shape[1])
        turn = lax.broadcasted_iota(jnp.int32, shape, 0) == jnp.broadcast_to(point >> (cols.bit_length() - 1), shape)
        turn = turn.astype(F32).astype(BF16)
        wave[r] = sum(jnp.dot(phase[i], turn, preferred_element_type=F32) for i in range(2))


def tables(points, phases, cols):
    targets, own = 2 * points[0].shape[0], points[0].shape[1]
    return pl.pallas_call(
        tables_kernel,
        out_shape=[
            jax.ShapeDtypeStruct((targets, cols, own), BF16),
            jax.ShapeDtypeStruct((targets, phases.shape[2], own), F32),
        ],
        compiler_params=pltpu.CompilerParams(vmem_limit_bytes=16 * 1024 * 1024),
        cost_estimate=pl.CostEstimate(flops=0, bytes_accessed=3 * targets * cols * own, transcendentals=0),
        name="tables",
    )(*points, phases)


def front_kernel(sources, find, blocks, source_of, *refs):
    parts_in, refs = refs[:sources], refs[sources:]
    cond, ytab, ztab, pick, wave, even, odd, vals, mixed, section, arrived = refs
    conds, groups = cond.shape[0], cond.shape[1]
    cols = pick.shape[1]
    own_y = cols // KF
    classes = ztab.shape[0]
    each = KF // classes
    count = vals.shape[0]
    for f in range(count):
        wanted, inside = find(blocks, source_of, f)
        for s in range(sources):
            @pl.when(wanted == s)
            def _(f=f, s=s):
                pltpu.make_async_copy(parts_in[s].at[inside], vals.at[f], arrived.at[f]).start()

    units = [(pair, group) for pair in range(conds // 2) for group in range(groups)]
    rows = 2 * each

    def sections(now, carry):
        pltpu.make_async_copy(parts_in[0].at[0], vals.at[now], arrived.at[now]).wait()
        for first in range(0, len(units), 2):
            two = units[first:first + 2]
            density = [
                jnp.concatenate([vals[now, group] * cond[2 * pair + i, group] for pair, group in two], axis=1) for i in range(2)
            ]
            out = jnp.dot(ytab[...], jnp.concatenate(density, axis=0), preferred_element_type=F32).astype(BF16)
            for i, (pair, group) in enumerate(two):
                at = (group * conds + 2 * pair) * each
                for kind in range(classes):
                    for half in range(2):
                        base = (half * classes + kind) * rows
                        mixed[kind, at:at + rows, half * LANES:half * LANES + LANES] = out[base:base + rows, i * LANES:i * LANES + LANES]
        for kind in range(classes):
            value = jnp.dot(mixed[kind], ztab[kind], preferred_element_type=F32)
            section[now, 2 * kind] = value[:, :128]
            section[now, 2 * kind + 1] = value[:, 128:]
        return carry

    lax.fori_loop(0, count, sections, 0)
    place = lax.broadcasted_iota(jnp.int32, (conds, 128), 1) // KF
    planes_in = [(group, half) for group in range(groups) for half in range(2)]

    def rows_of(f, kind, half, group, k):
        return section[f, 2 * kind + half, pl.ds(group * conds * each + k, conds, stride=each), :]

    def pieces_of(f, target):
        if classes == 1:
            parts = []
            for group, half in planes_in:
                rows = [rows_of(f, 0, half, group, target * own_y + y) for y in range(own_y)]
                for piece in range(4):
                    cut = slice(KF * piece, KF * piece + KF)
                    parts.append(jnp.concatenate([row[:, cut] for row in rows], axis=1))
            return parts
        found = {}
        loaded = [[rows_of(f, kind, half, group, target) for kind in range(classes)] for group, half in planes_in]
        for piece in range(4):
            merged = []
            for rows in loaded:
                value = rows[-piece % 4]
                for slot in range(1, 4):
                    value = jnp.where(place == slot, rows[(slot - piece) % 4], value)
                merged.append(value)
            turned = jnp.concatenate(merged, axis=0)
            if piece:
                turned = pltpu.roll(turned, 128 - KF * piece, 1)
            for i in range(len(planes_in)):
                found[4 * i + piece] = turned[i * conds:(i + 1) * conds]
        return [found[i] for i in range(4 * len(planes_in))]

    def folded(f, target):
        parts = pieces_of(f, target)
        planes_count = len(parts) // 2
        out = []
        for x in range(planes_count // 2):
            high = planes_count - 1 - x
            out += [parts[2 * high + i] + parts[2 * x + i] for i in range(2)]
            out += [parts[2 * high + i] - parts[2 * x + i] for i in range(2)]
        return out

    def one_target(step, parity, out_ref):
        order = target_of(step, pick.shape[0]) + parity
        target = lax.axis_index("grid").astype(jnp.int32) ^ order
        parts = [folded(f, target) for f in range(count)]
        lines = XG * groups // 2
        left = jnp.concatenate([p for part in parts for p in part], axis=0).astype(BF16)
        found = jnp.dot(left, pick[order], preferred_element_type=F32)
        turn = [wave[order, i:i + 1, :] for i in range(2 * lines + 2)]
        for f in range(count):
            real = imag = None
            for x in range(lines):
                cosine, sine = turn[x], turn[lines + x]
                base = 4 * (f * lines + x) * conds
                sum_re, sum_im, diff_re, diff_im = (found[base + i * conds:base + (i + 1) * conds] for i in range(4))
                add_real = sum_re * cosine + diff_im * sine
                add_imag = sum_im * cosine - diff_re * sine
                real = add_real if real is None else real + add_real
                imag = add_imag if imag is None else imag + add_imag
            cosine, sine = turn[2 * lines], turn[2 * lines + 1]
            both = [real * cosine + imag * sine, imag * cosine - real * sine]
            out_ref[step, 2 * conds * f:2 * conds * f + 2 * conds, :] = jnp.concatenate(both, axis=0).astype(BF16)

    def body(step, carry):
        one_target(step, 0, even)
        one_target(step, 1, odd)
        return carry

    lax.fori_loop(0, even.shape[0], body, 0)


def front(find, count, blocks, sources, cond, ytab, ztab, pick, wave):
    conds, groups = cond.shape[:2]
    targets, cols, own = pick.shape
    classes = ztab.shape[0]
    rows = 2 * conds
    shape = jax.ShapeDtypeStruct((targets // 2, count * rows, own), BF16)
    inside, scalars = pl.BlockSpec(memory_space=pltpu.VMEM), pl.BlockSpec(memory_space=pltpu.SMEM)
    return pl.pallas_call(
        functools.partial(front_kernel, len(sources), find),
        in_specs=[scalars] * 2 + [pl.BlockSpec(memory_space=pl.ANY)] * len(sources) + [inside] * 5,
        out_specs=[inside] * 2,
        scratch_shapes=[
            pltpu.VMEM((count,) + cond.shape[1:], BF16),
            pltpu.VMEM((classes, groups * conds * KF // classes, 2 * LANES), BF16),
            pltpu.VMEM((count, 2 * classes, groups * conds * KF // classes, XG * KF), F32),
            pltpu.SemaphoreType.DMA((count,)),
        ],
        out_shape=[shape, shape],
        compiler_params=pltpu.CompilerParams(vmem_limit_bytes=FRONT_VMEM),
        cost_estimate=pl.CostEstimate(flops=count * 900_000_000, bytes_accessed=count * 2_000_000, transcendentals=0),
        name="front",
    )(blocks, jnp.asarray(SOURCES.reshape(-1), jnp.int32), *sources, cond, ytab, ztab, pick, wave)


def screen_kernel(split, here, *refs):
    *pieces, w_even, w_odd, even, odd, side = refs

    @pl.when(pl.program_id(0) == 0)
    def _():
        first = 0
        for i, count in enumerate(split):
            group = pieces[sum(split[:i]):sum(split[:i]) + count]
            total = group[0][...].astype(F32)
            for piece in group[1:]:
                total = total + piece[...].astype(F32)
            side[first:first + total.shape[0], :] = total.astype(BF16)
            first += total.shape[0]

    even[0] = jnp.dot(side[...], w_even[...], preferred_element_type=F32).astype(BF16)
    odd[0] = jnp.dot(side[...], w_odd[...], preferred_element_type=F32).astype(BF16)


def screen(here, parts, screened, targets):
    own = parts[0][0].shape[1]
    rows = sum(p[0].shape[0] for p in parts)
    flat = [piece for part in parts for piece in part]
    if own % 128:
        side = jnp.concatenate([sum(p.astype(F32) for p in part) for part in parts], axis=0).astype(BF16)
        part = jnp.dot(side, screened, preferred_element_type=F32).astype(BF16)
        part = jnp.transpose(part.reshape(rows, targets, own), (1, 0, 2))
        even = here[0] ^ target_of(jnp.arange(targets // 2, dtype=jnp.int32), targets)
        return jnp.take(part, even, axis=0), jnp.take(part, even ^ 1, axis=0)
    shape = jax.ShapeDtypeStruct((targets // 2, rows, own), BF16)
    spec = pltpu.PrefetchScalarGridSpec(
        num_scalar_prefetch=1,
        grid=(targets // 2,),
        in_specs=[pl.BlockSpec(x.shape, lambda r, h: (0, 0)) for x in flat] + [
            pl.BlockSpec((own, own), lambda r, h: (0, h[0] ^ target_of(r, targets))),
            pl.BlockSpec((own, own), lambda r, h: (0, h[0] ^ target_of(r, targets) ^ 1)),
        ],
        out_specs=[pl.BlockSpec((1, rows, own), lambda r, h: (r, 0, 0))] * 2,
        scratch_shapes=[pltpu.VMEM((rows, own), BF16)],
    )
    return pl.pallas_call(
        functools.partial(screen_kernel, [len(p) for p in parts]),
        grid_spec=spec,
        out_shape=[shape, shape],
        compiler_params=pltpu.CompilerParams(vmem_limit_bytes=WHOLE_VMEM),
        cost_estimate=pl.CostEstimate(flops=2 * rows * own * own * targets, bytes_accessed=2 * own * own * targets, transcendentals=0),
        name="screen",
    )(here, *flat, screened, screened)


def close_kernel(split, place, blocks, slot_of, *refs):
    ins, outs, sums = refs[:sum(map(sum, split))], refs[sum(map(sum, split)):-2], refs[-2:]
    chunks, functions, unit, _ = sums[0].shape
    half = unit // 2
    for side, pieces in enumerate(split):
        first = 0
        for count in pieces:
            group, ins = ins[:count], ins[count:]
            here = group[0].shape[1] // unit
            for chunk in range(chunks):
                total = group[0][chunk].astype(F32)
                for piece in group[1:]:
                    total = total + piece[chunk].astype(F32)
                sums[side][chunk, first:first + here] = total.reshape(here, unit, total.shape[1])
            first += here
    slots = [[place(blocks, slot_of, side, f) for f in range(functions)] for side in range(2)]
    product = None
    for chunk in range(chunks):
        for part in range(2):
            rows = slice(half * part, half * part + half)
            left, right = (
                jnp.concatenate([sums[side][chunk, slot][rows] for slot in slots[side]], axis=0).astype(BF16) for side in range(2)
            )
            term = lax.dot_general(left, right, (((1,), (1,)), ((), ())), preferred_element_type=F32)
            product = term if product is None else product + term
    if len(outs) == 1:
        outs[0][...] = product
    else:
        steps, rows = outs[0].shape[:2]
        for step in range(steps):
            for parity in range(2):
                first = (target_of(step, 2 * steps) + parity) * rows
                outs[parity][step] = product[first:first + rows]


def close(place, blocks, u_parts, b_parts, conds, targets, by_target):
    split = [[len(p) for p in side] for side in (u_parts, b_parts)]
    flat = [x for side in (u_parts, b_parts) for p in side for x in p]
    functions = BLK
    rows = functions * conds
    chunks, _, own = flat[0].shape
    if by_target:
        out = [jax.ShapeDtypeStruct((targets // 2, rows // targets, rows), F32)] * 2
    else:
        out = [jax.ShapeDtypeStruct((rows, rows), F32)]
    spec = pltpu.PrefetchScalarGridSpec(
        num_scalar_prefetch=2,
        grid=(1,),
        in_specs=[pl.BlockSpec(x.shape, lambda i, b, t: (0, 0, 0)) for x in flat],
        out_specs=[pl.BlockSpec(o.shape, lambda i, b, t, o=o: (0,) * len(o.shape)) for o in out],
        scratch_shapes=[pltpu.VMEM((chunks, functions, 2 * conds, own), F32)] * 2,
    )
    return pl.pallas_call(
        functools.partial(close_kernel, split, place),
        grid_spec=spec,
        out_shape=out,
        cost_estimate=pl.CostEstimate(flops=4 * rows * rows * own, bytes_accessed=8 * rows * own, transcendentals=0),
        compiler_params=pltpu.CompilerParams(vmem_limit_bytes=24 * 1024 * 1024),
        name="close",
    )(blocks, jnp.asarray(slots_of().reshape(-1), jnp.int32), *flat)


def swap(array, axis, mask, size):
    return lax.ppermute(array, axis, [(i, i ^ mask) for i in range(size)])


def target_of(step, targets):
    bits = (targets // 2).bit_length() - 1
    return 2 * sum(((step >> i) & 1) << (bits - 1 - i) for i in range(bits))


def after(value, *others):
    return lax.optimization_barrier((value, *others))[0]


def add(left, right):
    return (left.astype(F32) + right.astype(F32)).astype(left.dtype)


def halve(kept, got, mask, targets):
    half = kept.shape[0] // 2
    sent = add(kept[half:], got[half:])
    return add(kept[:half], got[:half]), swap(sent, "grid", mask, targets), sent


def halving(even, odd, targets):
    got = swap(odd, "grid", 1, targets)
    mask = 2
    while even.shape[0] > 1:
        even, got, _ = halve(even, got, mask, targets)
        mask *= 2
    return [even[0], got[0]]


def both_blocks(kept, got, targets):
    total = add(kept, got)
    come = swap(total, "grid", targets // 2, targets)
    return [total, come[::-1]]


def round_ring(own, holder, size, reverse):
    order = list(range(size))
    if reverse:
        order = order[::-1]
    pairs = [(order[i], order[(i + 1) % size]) for i in range(size)]
    place = [0] * size
    for i, device in enumerate(order):
        place[device] = i
    place = jnp.array(place, jnp.int32)
    away = (place[lax.axis_index("band")] - place[holder]) % size
    chunks = len(own)
    got = []
    for step in range(chunks + size - 2):
        mine = own[min(step, chunks - 1)]
        sent = mine if step == 0 else jnp.where(away == 0, mine, got[-1])
        got.append(lax.ppermute(sent, "band", pairs))
    out = []
    for j in range(chunks):
        value = own[j]
        for hop in range(1, size):
            value = jnp.where(away == hop, got[j + hop - 1], value)
        out.append(value)
    return out


def by_ring(valence, blocks, side, held, size):
    half = BLK // 2
    own = planes(valence, blocks, [lambda b, j=j: b[side] % held * BLK + j for j in range(BLK)], 1)
    right = round_ring(own[:half], blocks[side] // held, size, False)
    left = round_ring(own[half:], blocks[side] // held, size, True)
    return right, left


class Swaps:
    def __init__(self, own, owner):
        self.own, self.owner = own, owner
        self.got = [(own[0], own[1])]
        self.sent = [(own[0], own[1])]

    def send(self):
        across, along = self.sent[-1]
        self.got.append((swap(across, "band", 1, 4), swap(along, "band", 2, 4)))

    def choose(self):
        x, y = self.got[-1]
        ahead = (2, 3) if len(self.got) == 2 else (3, 2)
        self.sent.append(tuple(jnp.where(self.owner, self.own[q], a) for q, a in zip(ahead, (y, x), strict=True)))

    def sources(self, late):
        if late:
            return [*self.own[2:], *self.got[3]]
        return [*self.own[:2], *self.got[1], *self.got[2]]


def per_device(sizes, valence, conduction, screened, blocks, gsphere):
    n_band, n_grid = sizes
    held = valence.shape[0] // BLK
    conds, own = conduction.shape[0], gsphere.shape[0]
    cols = KF // n_grid * KF
    half, quarter = BLK // 2, BLK // 4
    swaps = n_band == 4
    at = lax.axis_index("grid").astype(jnp.int32)[None]
    cosine, sine = fourier_parts(GRID_N, KF)
    classes = classes_of(cols // KF)
    ytab, ztab = (jnp.asarray(t(cosine, sine, classes)) for t in (y_table, z_table))

    def role(b, side):
        return lax.axis_index("band").astype(jnp.int32) ^ (b[side] // held)

    def quarters(wanted, stay=False):
        firsts = [lambda b, s=s, q=q: b[s] % held * BLK + quarter * q for s, q in wanted]
        return planes(valence, blocks, firsts, quarter, stay)

    def more(points, i):
        return jnp.concatenate([points, swap(points, "grid", 1 << i, n_grid)], axis=0)

    points = gsphere.reshape(1, own)
    levels = n_grid.bit_length() - 1
    if swaps:
        own_a = quarters([(0, 0), (0, 1)], True)
        own_b = quarters([(1, 0), (1, 1), (0, 2), (0, 3), (1, 2), (1, 3)])
        a, b = (
            Swaps(o, lax.axis_index("band") == blocks[s] // held)
            for s, o in enumerate(([*own_a, *own_b[2:4]], [*own_b[:2], *own_b[4:]]))
        )
        a.send()
        a.choose()
        a.send()
        b.send()
        a.choose()
        a.send()
        points = after(points, *a.sent[1])
        conduction = after(conduction, *a.sent[1])
        for i in range(levels - 1):
            points = more(points, i)
        last = swap(points, "grid", n_grid // 2, n_grid)
        sources = lambda side, late: (a, b)[side].sources(late)
    else:
        rings = [by_ring(valence, blocks, s, held, n_band) for s in range(2)]
        sources = lambda side, late: rings[side][late]
        for i in range(levels - 1):
            points = more(points, i)
        last = swap(points, "grid", n_grid // 2, n_grid)
    cond, = planes(conduction, blocks, [lambda b: 0], conds)
    pick, wave = tables([points, last], jnp.asarray(x_phases(n_grid)), cols)

    def part(side, late, *others):
        def find(b, source_of, f):
            if not swaps:
                return f, 0
            return source_of[role(b, side) * 4 + 2 * late + f // quarter], f % quarter
        return front(find, half, after(blocks, *others), sources(side, late), cond, ytab, ztab, pick, wave)

    def core(pair):
        return pair[0], swap(pair[1], "grid", 1, n_grid)

    early_a = core(part(0, 0, *(a.sent[2] if swaps else ())))
    if swaps:
        b.got[1] = lax.optimization_barrier((*b.got[1], early_a[0]))[:2]
        b.choose()
        b.send()
    early_a = halve(*early_a, 2, n_grid)
    late_a = core(part(0, 1, early_a[2]))
    late_a = halve(*late_a, 2, n_grid)
    if swaps:
        b.choose()
        b.send()
    early_b = core(part(1, 0, late_a[2], *(b.sent[2] if swaps else ())))
    side_a = [after(early_a[0], early_b[0]), early_a[1]], [late_a[0], late_a[1]]
    side_a = [jnp.concatenate([e, l], axis=1) for e, l in zip(*side_a, strict=True)]
    side_a = halve(*side_a, 4, n_grid)
    late_b = core(part(1, 1, side_a[2]))
    early_b = halve(*early_b, 2, n_grid)

    def finish(pair, mask):
        pair = pair[:2]
        while pair[0].shape[0] > 1:
            pair = halve(*pair, mask, n_grid)[:2]
            mask *= 2
        return [p[0] for p in pair]

    def until_two(pair, mask):
        pair = pair[:2]
        while pair[0].shape[0] > 2:
            pair = halve(*pair, mask, n_grid)[:2]
            mask *= 2
        return pair

    side_a = [finish(side_a, 8)]
    part_u = screen(after(at, late_b[0]), side_a, screened, n_grid)
    late_b = until_two((after(late_b[0], part_u[0]), late_b[1]), 2)
    part_u = until_two(core(part_u), 2)
    side_b = [both_blocks(*until_two(early_b, 4), n_grid), both_blocks(*late_b, n_grid)]

    by_target = n_grid == BLK

    def place(b, slot_of, side, f):
        if side == 0 and by_target:
            f = f ^ lax.axis_index("grid").astype(jnp.int32)
        return slot_of[role(b, side) * BLK + f] if swaps else f

    shares = close(place, blocks, [part_u], side_b, conds, n_grid, by_target)
    if not by_target:
        share = shares[0].reshape(n_grid, -1, shares[0].shape[1])
        even = at ^ target_of(jnp.arange(n_grid // 2, dtype=jnp.int32), n_grid)
        shares = jnp.take(share, even, axis=0), jnp.take(share, even ^ 1, axis=0)
    return sum(halving(*shares, n_grid))[None]


def solution(mesh):
    sizes = (mesh.shape["band"], mesh.shape["grid"])
    in_specs = (P("band", "grid", None), P("band", "grid", None), P("grid", None), P(), P("grid"))
    out_specs = P("band", "grid", None)
    return jax.shard_map(
        functools.partial(per_device, sizes), mesh=mesh, in_specs=in_specs, out_specs=out_specs, check_vma=False
    )
```

```python
import functools
import math

import jax
import jax.numpy as jnp
import numpy as np
from jax import lax
from jax.experimental import pallas as pl
from jax.experimental.pallas import tpu as pltpu
from jax.sharding import PartitionSpec as P

GRID_N = 96
KF = 32
BLK = 8
XG = 4
LANES = XG * GRID_N
F32 = jnp.float32
BF16 = jnp.bfloat16
WHOLE_VMEM = 56 * 1024 * 1024
PART_VMEM = 20 * 1024 * 1024
FRONT_VMEM = 24 * 1024 * 1024


def fourier_parts(length, kept):
    phase = np.arange(length)[:, None] * (np.arange(kept) - kept // 2)[None, :] % length * (2.0 * math.pi / length)
    return (np.cos(phase) / math.sqrt(length)).astype(BF16), (np.sin(phase) / math.sqrt(length)).astype(BF16)


def classes_of(own_y):
    return XG if own_y == XG else 1


def y_table(cosine, sine, classes):
    order = np.arange(GRID_N).reshape(-1, XG).T.reshape(-1)
    one = np.stack([cosine[order].T, -sine[order].T]).reshape(2, KF // classes, classes, GRID_N)
    table = np.zeros((2, classes, 2, KF // classes, 2, GRID_N), BF16)
    for pair in range(2):
        table[:, :, pair, :, pair] = one.transpose(0, 2, 1, 3)
    return table.reshape(4 * KF, 2 * GRID_N)


def z_table(cosine, sine, classes):
    both = np.stack([np.stack([cosine, -sine], axis=1), np.stack([sine, cosine], axis=1)])
    table = np.zeros((2, XG, GRID_N, XG, 2, KF), BF16)
    for x in range(XG):
        table[:, x, :, x] = both
    table = table.reshape(2 * LANES, 2, 4, KF)
    return np.stack([np.roll(table, i, axis=2).reshape(2 * LANES, XG * 2 * KF) for i in range(classes)])


def x_phases(n_grid):
    slab = GRID_N // n_grid
    lines = -(-slab // XG) * XG // 2
    freqs = 2.0 * math.pi / GRID_N * (np.arange(KF) - KF // 2)
    away = (lines - 0.5 - np.arange(lines))[:, None] * freqs
    middle = (slab * np.arange(n_grid) + lines - 0.5)[:, None, None] * freqs
    scale = 1.0 / math.sqrt(GRID_N)
    fixed = np.broadcast_to(np.concatenate([np.cos(away), np.sin(away)]), (n_grid, 2 * lines, KF))
    rows = np.concatenate([fixed, np.cos(middle) * scale, np.sin(middle) * scale], axis=1)
    rows = np.pad(rows, ((0, 0), (0, -rows.shape[1] % 8), (0, 0)))
    high = rows.astype(BF16)
    return np.stack([high, (rows - high.astype(np.float64)).astype(BF16)], axis=1)


HOLDS = np.array([[0, 1, 3, 2], [0, 2, 3, 1], [1, 3, 0, 2], [1, 0, 3, 2]])
SOURCES = np.array([[0, 1, 1, 0], [2, 4, 2, 3], [3, 5, 2, 3], [4, 5, 2, 3]])


def slots_of():
    quarter = BLK // 4
    return np.argsort((quarter * HOLDS[:, :, None] + np.arange(quarter)).reshape(4, BLK), axis=1)


def planes_kernel(firsts, blocks, src, *refs):
    outs, (rows, held, arrived) = refs[:-3], refs[-3:]
    groups, together = outs[0].shape[1], held.shape[0] // outs[0].shape[1]
    functions = src.shape[1]
    tiles, high = LANES // 128, GRID_N // XG

    def fetch(group):
        part = pl.ds(together * group, together)
        return pltpu.make_async_copy(src.at[part], held.at[part], arrived.at[group])

    for group in range(groups):
        fetch(group).start()
    for group in range(groups):
        fetch(group).wait()
        for x in range(together):
            for y in range(high):
                for t in range(tiles):
                    cut = slice(y * LANES + 128 * t, y * LANES + 128 * t + 128)
                    rows[x * tiles + t, y * functions:(y + 1) * functions, :] = held[together * group + x, :, cut].astype(F32)
        for first, out in zip(firsts, outs, strict=True):
            for f in range(out.shape[0]):
                at = pl.ds(first(blocks) + f, high, stride=functions)
                wide = [jnp.concatenate([rows[x * tiles + t, at, :] for t in range(tiles)], axis=1) for x in range(together)]
                wide += [jnp.zeros((high, LANES), F32)] * (XG - together)
                lines = [
                    jnp.concatenate([w[:, GRID_N * low:GRID_N * low + GRID_N] for w in wide], axis=1) for low in range(XG)
                ]
                out[f, group] = jnp.concatenate(lines, axis=0).astype(BF16)


def planes(orbitals, blocks, firsts, count, stay=False):
    orbitals = jnp.transpose(orbitals, (1, 0, 2))
    slab, functions, size = orbitals.shape
    together = min(XG, slab)
    groups = slab // together
    shape = (count, groups, GRID_N, LANES)
    spec = pltpu.PrefetchScalarGridSpec(
        num_scalar_prefetch=1,
        grid=(1,),
        in_specs=[pl.BlockSpec(memory_space=pl.ANY)],
        out_specs=[pl.BlockSpec(shape, lambda g, b: (0, 0, 0, 0))] * len(firsts),
        scratch_shapes=[
            pltpu.VMEM((LANES // 128 * together, GRID_N // XG * functions, 128), F32),
            pltpu.VMEM((slab, functions, size), BF16),
            pltpu.SemaphoreType.DMA((groups,)),
        ],
    )
    return pl.pallas_call(
        functools.partial(planes_kernel, firsts),
        grid_spec=spec,
        out_shape=[jax.ShapeDtypeStruct(shape, BF16)] * len(firsts),
        compiler_params=pltpu.CompilerParams(vmem_limit_bytes=WHOLE_VMEM if stay else PART_VMEM),
        cost_estimate=pl.CostEstimate(flops=0, bytes_accessed=4 * slab * functions * size, transcendentals=0),
        name="planes",
    )(blocks, orbitals)


def tables_kernel(*refs):
    *points, phases, pick, wave = refs
    cols = pick.shape[1]
    phase = phases[lax.axis_index("grid")]
    for r in range(pick.shape[0]):
        half = points[0].shape[0]
        point = points[r // half][r % half:r % half + 1, :]
        shape = (cols, point.shape[1])
        found = lax.broadcasted_iota(jnp.int32, shape, 0) == jnp.broadcast_to(point & (cols - 1), shape)
        pick[r] = found.astype(F32).astype(BF16)
        shape = (KF, point.shape[1])
        turn = lax.broadcasted_iota(jnp.int32, shape, 0) == jnp.broadcast_to(point >> (cols.bit_length() - 1), shape)
        turn = turn.astype(F32).astype(BF16)
        wave[r] = sum(jnp.dot(phase[i], turn, preferred_element_type=F32) for i in range(2))


def tables(points, phases, cols):
    targets, own = 2 * points[0].shape[0], points[0].shape[1]
    return pl.pallas_call(
        tables_kernel,
        out_shape=[
            jax.ShapeDtypeStruct((targets, cols, own), BF16),
            jax.ShapeDtypeStruct((targets, phases.shape[2], own), F32),
        ],
        compiler_params=pltpu.CompilerParams(vmem_limit_bytes=16 * 1024 * 1024),
        cost_estimate=pl.CostEstimate(flops=0, bytes_accessed=3 * targets * cols * own, transcendentals=0),
        name="tables",
    )(*points, phases)


def front_kernel(sources, find, blocks, source_of, *refs):
    parts_in, refs = refs[:sources], refs[sources:]
    cond, ytab, ztab, pick, wave, even, odd, vals, mixed, section, arrived = refs
    conds, groups = cond.shape[0], cond.shape[1]
    cols = pick.shape[1]
    own_y = cols // KF
    classes = ztab.shape[0]
    each = KF // classes
    count = vals.shape[0]
    for f in range(count):
        wanted, inside = find(blocks, source_of, f)
        for s in range(sources):
            @pl.when(wanted == s)
            def _(f=f, s=s):
                pltpu.make_async_copy(parts_in[s].at[inside], vals.at[f], arrived.at[f]).start()

    units = [(pair, group) for pair in range(conds // 2) for group in range(groups)]
    rows = 2 * each

    def sections(now, carry):
        pltpu.make_async_copy(parts_in[0].at[0], vals.at[now], arrived.at[now]).wait()
        for first in range(0, len(units), 2):
            two = units[first:first + 2]
            density = [
                jnp.concatenate([vals[now, group] * cond[2 * pair + i, group] for pair, group in two], axis=1) for i in range(2)
            ]
            out = jnp.dot(ytab[...], jnp.concatenate(density, axis=0), preferred_element_type=F32).astype(BF16)
            for i, (pair, group) in enumerate(two):
                at = (group * conds + 2 * pair) * each
                for kind in range(classes):
                    for half in range(2):
                        base = (half * classes + kind) * rows
                        mixed[kind, at:at + rows, half * LANES:half * LANES + LANES] = out[base:base + rows, i * LANES:i * LANES + LANES]
        for kind in range(classes):
            value = jnp.dot(mixed[kind], ztab[kind], preferred_element_type=F32)
            section[now, 2 * kind] = value[:, :128]
            section[now, 2 * kind + 1] = value[:, 128:]
        return carry

    lax.fori_loop(0, count, sections, 0)
    place = lax.broadcasted_iota(jnp.int32, (conds, 128), 1) // KF
    planes_in = [(group, half) for group in range(groups) for half in range(2)]

    def rows_of(f, kind, half, group, k):
        return section[f, 2 * kind + half, pl.ds(group * conds * each + k, conds, stride=each), :]

    def pieces_of(f, target):
        if classes == 1:
            parts = []
            for group, half in planes_in:
                rows = [rows_of(f, 0, half, group, target * own_y + y) for y in range(own_y)]
                for piece in range(4):
                    cut = slice(KF * piece, KF * piece + KF)
                    parts.append(jnp.concatenate([row[:, cut] for row in rows], axis=1))
            return parts
        found = {}
        loaded = [[rows_of(f, kind, half, group, target) for kind in range(classes)] for group, half in planes_in]
        for piece in range(4):
            merged = []
            for rows in loaded:
                value = rows[-piece % 4]
                for slot in range(1, 4):
                    value = jnp.where(place == slot, rows[(slot - piece) % 4], value)
                merged.append(value)
            turned = jnp.concatenate(merged, axis=0)
            if piece:
                turned = pltpu.roll(turned, 128 - KF * piece, 1)
            for i in range(len(planes_in)):
                found[4 * i + piece] = turned[i * conds:(i + 1) * conds]
        return [found[i] for i in range(4 * len(planes_in))]

    def folded(f, target):
        parts = pieces_of(f, target)
        planes_count = len(parts) // 2
        out = []
        for x in range(planes_count // 2):
            high = planes_count - 1 - x
            out += [parts[2 * high + i] + parts[2 * x + i] for i in range(2)]
            out += [parts[2 * high + i] - parts[2 * x + i] for i in range(2)]
        return out

    def one_target(step, parity, out_ref):
        order = target_of(step, pick.shape[0]) + parity
        target = lax.axis_index("grid").astype(jnp.int32) ^ order
        parts = [folded(f, target) for f in range(count)]
        lines = XG * groups // 2
        left = jnp.concatenate([p for part in parts for p in part], axis=0).astype(BF16)
        found = jnp.dot(left, pick[order], preferred_element_type=F32)
        turn = [wave[order, i:i + 1, :] for i in range(2 * lines + 2)]
        for f in range(count):
            real = imag = None
            for x in range(lines):
                cosine, sine = turn[x], turn[lines + x]
                base = 4 * (f * lines + x) * conds
                sum_re, sum_im, diff_re, diff_im = (found[base + i * conds:base + (i + 1) * conds] for i in range(4))
                add_real = sum_re * cosine + diff_im * sine
                add_imag = sum_im * cosine - diff_re * sine
                real = add_real if real is None else real + add_real
                imag = add_imag if imag is None else imag + add_imag
            cosine, sine = turn[2 * lines], turn[2 * lines + 1]
            both = [real * cosine + imag * sine, imag * cosine - real * sine]
            out_ref[step, 2 * conds * f:2 * conds * f + 2 * conds, :] = jnp.concatenate(both, axis=0).astype(BF16)

    def body(step, carry):
        one_target(step, 0, even)
        one_target(step, 1, odd)
        return carry

    lax.fori_loop(0, even.shape[0], body, 0)


def front(find, count, blocks, sources, cond, ytab, ztab, pick, wave):
    conds, groups = cond.shape[:2]
    targets, cols, own = pick.shape
    classes = ztab.shape[0]
    rows = 2 * conds
    shape = jax.ShapeDtypeStruct((targets // 2, count * rows, own), BF16)
    inside, scalars = pl.BlockSpec(memory_space=pltpu.VMEM), pl.BlockSpec(memory_space=pltpu.SMEM)
    return pl.pallas_call(
        functools.partial(front_kernel, len(sources), find),
        in_specs=[scalars] * 2 + [pl.BlockSpec(memory_space=pl.ANY)] * len(sources) + [inside] * 5,
        out_specs=[inside] * 2,
        scratch_shapes=[
            pltpu.VMEM((count,) + cond.shape[1:], BF16),
            pltpu.VMEM((classes, groups * conds * KF // classes, 2 * LANES), BF16),
            pltpu.VMEM((count, 2 * classes, groups * conds * KF // classes, XG * KF), F32),
            pltpu.SemaphoreType.DMA((count,)),
        ],
        out_shape=[shape, shape],
        compiler_params=pltpu.CompilerParams(vmem_limit_bytes=FRONT_VMEM),
        cost_estimate=pl.CostEstimate(flops=count * 900_000_000, bytes_accessed=count * 2_000_000, transcendentals=0),
        name="front",
    )(blocks, jnp.asarray(SOURCES.reshape(-1), jnp.int32), *sources, cond, ytab, ztab, pick, wave)


def screen_kernel(split, parity, *refs):
    *pieces, screened, out = refs
    sums = []
    for i, count in enumerate(split):
        group = pieces[sum(split[:i]):sum(split[:i]) + count]
        total = group[0][...].astype(F32)
        for piece in group[1:]:
            total = total + piece[...].astype(F32)
        sums.append(total.astype(BF16))
    side = jnp.concatenate(sums, axis=0)
    steps, _, own = out.shape
    here = lax.axis_index("grid").astype(jnp.int32)

    def step(r, carry):
        target = here ^ target_of(r, 2 * steps) ^ parity
        columns = screened[:, pl.ds(pl.multiple_of(target * own, own), own)]
        out[r] = jnp.dot(side, columns, preferred_element_type=F32).astype(BF16)
        return carry

    lax.fori_loop(0, steps, step, 0)


def screen(parts, screened, targets, parity):
    own = parts[0][0].shape[1]
    rows = sum(p[0].shape[0] for p in parts)
    flat = [piece for part in parts for piece in part]
    if own % 128:
        here = lax.axis_index("grid").astype(jnp.int32)
        side = jnp.concatenate([sum(p.astype(F32) for p in part) for part in parts], axis=0).astype(BF16)
        part = jnp.dot(side, screened, preferred_element_type=F32).astype(BF16)
        part = jnp.transpose(part.reshape(rows, targets, own), (1, 0, 2))
        wanted = here ^ target_of(jnp.arange(targets // 2, dtype=jnp.int32), targets) ^ parity
        return jnp.take(part, wanted, axis=0)
    inside = pl.BlockSpec(memory_space=pltpu.VMEM)
    return pl.pallas_call(
        functools.partial(screen_kernel, [len(p) for p in parts], parity),
        in_specs=[inside] * (len(flat) + 1),
        out_specs=inside,
        out_shape=jax.ShapeDtypeStruct((targets // 2, rows, own), BF16),
        compiler_params=pltpu.CompilerParams(vmem_limit_bytes=PART_VMEM),
        cost_estimate=pl.CostEstimate(flops=rows * own * own * targets, bytes_accessed=own * own * targets, transcendentals=0),
        name="screen",
    )(*flat, screened)


def close_kernel(split, place, blocks, slot_of, *refs):
    ins, outs, sums = refs[:sum(map(sum, split))], refs[sum(map(sum, split)):-2], refs[-2:]
    chunks, functions, unit, _ = sums[0].shape
    half = unit // 2
    for side, pieces in enumerate(split):
        first = 0
        for count in pieces:
            group, ins = ins[:count], ins[count:]
            here = group[0].shape[1] // unit
            for chunk in range(chunks):
                total = group[0][chunk].astype(F32)
                for piece in group[1:]:
                    total = total + piece[chunk].astype(F32)
                sums[side][chunk, first:first + here] = total.reshape(here, unit, total.shape[1])
            first += here
    slots = [[place(blocks, slot_of, side, f) for f in range(functions)] for side in range(2)]
    product = None
    for chunk in range(chunks):
        for part in range(2):
            rows = slice(half * part, half * part + half)
            left, right = (
                jnp.concatenate([sums[side][chunk, slot][rows] for slot in slots[side]], axis=0).astype(BF16) for side in range(2)
            )
            term = lax.dot_general(left, right, (((1,), (1,)), ((), ())), preferred_element_type=F32)
            product = term if product is None else product + term
    if len(outs) == 1:
        outs[0][...] = product
    else:
        steps, rows = outs[0].shape[:2]
        for step in range(steps):
            for parity in range(2):
                first = (target_of(step, 2 * steps) + parity) * rows
                outs[parity][step] = product[first:first + rows]


def close(place, blocks, u_parts, b_parts, conds, targets, by_target):
    split = [[len(p) for p in side] for side in (u_parts, b_parts)]
    flat = [x for side in (u_parts, b_parts) for p in side for x in p]
    functions = BLK
    rows = functions * conds
    chunks, _, own = flat[0].shape
    if by_target:
        out = [jax.ShapeDtypeStruct((targets // 2, rows // targets, rows), F32)] * 2
    else:
        out = [jax.ShapeDtypeStruct((rows, rows), F32)]
    spec = pltpu.PrefetchScalarGridSpec(
        num_scalar_prefetch=2,
        grid=(1,),
        in_specs=[pl.BlockSpec(x.shape, lambda i, b, t: (0, 0, 0)) for x in flat],
        out_specs=[pl.BlockSpec(o.shape, lambda i, b, t, o=o: (0,) * len(o.shape)) for o in out],
        scratch_shapes=[pltpu.VMEM((chunks, functions, 2 * conds, own), F32)] * 2,
    )
    return pl.pallas_call(
        functools.partial(close_kernel, split, place),
        grid_spec=spec,
        out_shape=out,
        cost_estimate=pl.CostEstimate(flops=4 * rows * rows * own, bytes_accessed=8 * rows * own, transcendentals=0),
        compiler_params=pltpu.CompilerParams(vmem_limit_bytes=24 * 1024 * 1024),
        name="close",
    )(blocks, jnp.asarray(slots_of().reshape(-1), jnp.int32), *flat)


def swap(array, axis, mask, size):
    return lax.ppermute(array, axis, [(i, i ^ mask) for i in range(size)])


def target_of(step, targets):
    bits = (targets // 2).bit_length() - 1
    return 2 * sum(((step >> i) & 1) << (bits - 1 - i) for i in range(bits))


def after(value, *others):
    return lax.optimization_barrier((value, *others))[0]


def add(left, right):
    return (left.astype(F32) + right.astype(F32)).astype(left.dtype)


def halve(kept, got, mask, targets):
    half = kept.shape[0] // 2
    sent = add(kept[half:], got[half:])
    return add(kept[:half], got[:half]), swap(sent, "grid", mask, targets), sent


def halving(even, odd, targets):
    got = swap(odd, "grid", 1, targets)
    mask = 2
    while even.shape[0] > 1:
        even, got, _ = halve(even, got, mask, targets)
        mask *= 2
    return [even[0], got[0]]


def both_blocks(kept, got, targets):
    total = add(kept, got)
    come = swap(total, "grid", targets // 2, targets)
    return [total, come[::-1]]


def round_ring(own, holder, size, reverse):
    order = list(range(size))
    if reverse:
        order = order[::-1]
    pairs = [(order[i], order[(i + 1) % size]) for i in range(size)]
    place = [0] * size
    for i, device in enumerate(order):
        place[device] = i
    place = jnp.array(place, jnp.int32)
    away = (place[lax.axis_index("band")] - place[holder]) % size
    chunks = len(own)
    got = []
    for step in range(chunks + size - 2):
        mine = own[min(step, chunks - 1)]
        sent = mine if step == 0 else jnp.where(away == 0, mine, got[-1])
        got.append(lax.ppermute(sent, "band", pairs))
    out = []
    for j in range(chunks):
        value = own[j]
        for hop in range(1, size):
            value = jnp.where(away == hop, got[j + hop - 1], value)
        out.append(value)
    return out


def by_ring(valence, blocks, side, held, size):
    half = BLK // 2
    own = planes(valence, blocks, [lambda b, j=j: b[side] % held * BLK + j for j in range(BLK)], 1)
    right = round_ring(own[:half], blocks[side] // held, size, False)
    left = round_ring(own[half:], blocks[side] // held, size, True)
    return right, left


class Swaps:
    def __init__(self, own, owner):
        self.own, self.owner = own, owner
        self.got = [(own[0], own[1])]
        self.sent = [(own[0], own[1])]

    def send(self):
        across, along = self.sent[-1]
        self.got.append((swap(across, "band", 1, 4), swap(along, "band", 2, 4)))

    def choose(self):
        x, y = self.got[-1]
        ahead = (2, 3) if len(self.got) == 2 else (3, 2)
        self.sent.append(tuple(jnp.where(self.owner, self.own[q], a) for q, a in zip(ahead, (y, x), strict=True)))

    def sources(self, late):
        if late:
            return [*self.own[2:], *self.got[3]]
        return [*self.own[:2], *self.got[1], *self.got[2]]


def per_device(sizes, valence, conduction, screened, blocks, gsphere):
    n_band, n_grid = sizes
    held = valence.shape[0] // BLK
    conds, own = conduction.shape[0], gsphere.shape[0]
    cols = KF // n_grid * KF
    half, quarter = BLK // 2, BLK // 4
    swaps = n_band == 4
    at = lax.axis_index("grid").astype(jnp.int32)[None]
    cosine, sine = fourier_parts(GRID_N, KF)
    classes = classes_of(cols // KF)
    ytab, ztab = (jnp.asarray(t(cosine, sine, classes)) for t in (y_table, z_table))

    def role(b, side):
        return lax.axis_index("band").astype(jnp.int32) ^ (b[side] // held)

    def quarters(wanted, stay=False):
        firsts = [lambda b, s=s, q=q: b[s] % held * BLK + quarter * q for s, q in wanted]
        return planes(valence, blocks, firsts, quarter, stay)

    def more(points, i):
        return jnp.concatenate([points, swap(points, "grid", 1 << i, n_grid)], axis=0)

    points = gsphere.reshape(1, own)
    levels = n_grid.bit_length() - 1
    if swaps:
        own_a = quarters([(0, 0), (0, 1)], True)
        own_b = quarters([(1, 0), (1, 1), (0, 2), (0, 3), (1, 2), (1, 3)])
        a, b = (
            Swaps(o, lax.axis_index("band") == blocks[s] // held)
            for s, o in enumerate(([*own_a, *own_b[2:4]], [*own_b[:2], *own_b[4:]]))
        )
        a.send()
        a.choose()
        a.send()
        b.send()
        a.choose()
        a.send()
        points = after(points, *a.sent[1])
        conduction = after(conduction, *a.sent[1])
        for i in range(levels - 1):
            points = more(points, i)
        last = swap(points, "grid", n_grid // 2, n_grid)
        sources = lambda side, late: (a, b)[side].sources(late)
    else:
        rings = [by_ring(valence, blocks, s, held, n_band) for s in range(2)]
        sources = lambda side, late: rings[side][late]
        for i in range(levels - 1):
            points = more(points, i)
        last = swap(points, "grid", n_grid // 2, n_grid)
    cond, = planes(conduction, blocks, [lambda b: 0], conds)
    pick, wave = tables([points, last], jnp.asarray(x_phases(n_grid)), cols)

    def part(side, late, *others):
        def find(b, source_of, f):
            if not swaps:
                return f, 0
            return source_of[role(b, side) * 4 + 2 * late + f // quarter], f % quarter
        return front(find, half, after(blocks, *others), sources(side, late), cond, ytab, ztab, pick, wave)

    def core(pair):
        return pair[0], swap(pair[1], "grid", 1, n_grid)

    early_a = core(part(0, 0, *(a.sent[2] if swaps else ())))
    if swaps:
        b.got[1] = lax.optimization_barrier((*b.got[1], early_a[0]))[:2]
        b.choose()
        b.send()
    early_a = halve(*early_a, 2, n_grid)
    late_a = core(part(0, 1, early_a[2]))
    late_a = halve(*late_a, 2, n_grid)
    if swaps:
        b.choose()
        b.send()
    early_b = core(part(1, 0, late_a[2], *(b.sent[2] if swaps else ())))
    side_a = [after(early_a[0], early_b[0]), early_a[1]], [late_a[0], late_a[1]]
    side_a = [jnp.concatenate([e, l], axis=1) for e, l in zip(*side_a, strict=True)]
    side_a = halve(*side_a, 4, n_grid)
    early_b = halve(*early_b, 2, n_grid)
    late_b = core(part(1, 1, side_a[2], early_b[2]))

    def finish(pair, mask):
        pair = pair[:2]
        while pair[0].shape[0] > 1:
            pair = halve(*pair, mask, n_grid)[:2]
            mask *= 2
        return [p[0] for p in pair]

    def until_two(pair, mask):
        pair = pair[:2]
        while pair[0].shape[0] > 2:
            pair = halve(*pair, mask, n_grid)[:2]
            mask *= 2
        return pair

    side_a = [finish(side_a, 8)]
    early_b = both_blocks(*until_two(early_b, 4), n_grid)
    odd_u = screen([[after(side_a[0][0], late_b[0], early_b[0]), *side_a[0][1:]]], screened, n_grid, 1)
    late_b = halve(*late_b, 2, n_grid)
    even_u = screen([[after(side_a[0][0], odd_u, late_b[2]), *side_a[0][1:]]], screened, n_grid, 0)
    part_u = until_two(core((even_u, odd_u)), 2)
    side_b = [early_b, both_blocks(*until_two(late_b, 4), n_grid)]

    by_target = n_grid == BLK

    def place(b, slot_of, side, f):
        if side == 0 and by_target:
            f = f ^ lax.axis_index("grid").astype(jnp.int32)
        return slot_of[role(b, side) * BLK + f] if swaps else f

    shares = close(place, blocks, [part_u], side_b, conds, n_grid, by_target)
    if not by_target:
        share = shares[0].reshape(n_grid, -1, shares[0].shape[1])
        even = at ^ target_of(jnp.arange(n_grid // 2, dtype=jnp.int32), n_grid)
        shares = jnp.take(share, even, axis=0), jnp.take(share, even ^ 1, axis=0)
    share = add(shares[0], swap(shares[1], "grid", 1, n_grid))
    far = [swap(share[i], "grid", target_of(i, n_grid), n_grid) for i in range(1, n_grid // 2)]
    return sum(far, share[0])[None]


def solution(mesh):
    sizes = (mesh.shape["band"], mesh.shape["grid"])
    in_specs = (P("band", "grid", None), P("band", "grid", None), P("grid", None), P(), P("grid"))
    out_specs = P("band", "grid", None)
    return jax.shard_map(
        functools.partial(per_device, sizes), mesh=mesh, in_specs=in_specs, out_specs=out_specs, check_vma=False
    )
```

```python
import functools
import math

import jax
import jax.numpy as jnp
import numpy as np
from jax import lax
from jax.experimental import pallas as pl
from jax.experimental.pallas import tpu as pltpu
from jax.sharding import PartitionSpec as P

GRID_N = 96
KF = 32
BLK = 8
XG = 4
LANES = XG * GRID_N
F32 = jnp.float32
BF16 = jnp.bfloat16
WHOLE_VMEM = 56 * 1024 * 1024
PART_VMEM = 20 * 1024 * 1024
FRONT_VMEM = 24 * 1024 * 1024


def fourier_parts(length, kept):
    phase = np.arange(length)[:, None] * (np.arange(kept) - kept // 2)[None, :] % length * (2.0 * math.pi / length)
    return (np.cos(phase) / math.sqrt(length)).astype(BF16), (np.sin(phase) / math.sqrt(length)).astype(BF16)


def classes_of(own_y):
    return XG if own_y == XG else 1


def y_table(cosine, sine, classes):
    order = np.arange(GRID_N).reshape(-1, XG).T.reshape(-1)
    one = np.stack([cosine[order].T, -sine[order].T]).reshape(2, KF // classes, classes, GRID_N)
    table = np.zeros((2, classes, 2, KF // classes, 2, GRID_N), BF16)
    for pair in range(2):
        table[:, :, pair, :, pair] = one.transpose(0, 2, 1, 3)
    return table.reshape(4 * KF, 2 * GRID_N)


def z_table(cosine, sine, classes):
    both = np.stack([np.stack([cosine, -sine], axis=1), np.stack([sine, cosine], axis=1)])
    table = np.zeros((2, XG, GRID_N, XG, 2, KF), BF16)
    for x in range(XG):
        table[:, x, :, x] = both
    table = table.reshape(2 * LANES, 2, 4, KF)
    return np.stack([np.roll(table, i, axis=2).reshape(2 * LANES, XG * 2 * KF) for i in range(classes)])


def x_phases(n_grid):
    slab = GRID_N // n_grid
    lines = -(-slab // XG) * XG // 2
    freqs = 2.0 * math.pi / GRID_N * (np.arange(KF) - KF // 2)
    away = (lines - 0.5 - np.arange(lines))[:, None] * freqs
    middle = (slab * np.arange(n_grid) + lines - 0.5)[:, None, None] * freqs
    scale = 1.0 / math.sqrt(GRID_N)
    fixed = np.broadcast_to(np.concatenate([np.cos(away), np.sin(away)]), (n_grid, 2 * lines, KF))
    rows = np.concatenate([fixed, np.cos(middle) * scale, np.sin(middle) * scale], axis=1)
    rows = np.pad(rows, ((0, 0), (0, -rows.shape[1] % 8), (0, 0)))
    high = rows.astype(BF16)
    return np.stack([high, (rows - high.astype(np.float64)).astype(BF16)], axis=1)


HOLDS = np.array([[0, 1, 3, 2], [0, 2, 3, 1], [1, 3, 0, 2], [1, 0, 3, 2]])
SOURCES = np.array([[0, 1, 1, 0], [2, 4, 2, 3], [3, 5, 2, 3], [4, 5, 2, 3]])


def slots_of():
    quarter = BLK // 4
    return np.argsort((quarter * HOLDS[:, :, None] + np.arange(quarter)).reshape(4, BLK), axis=1)


def planes_kernel(firsts, blocks, src, *refs):
    outs, (rows, held, arrived) = refs[:-3], refs[-3:]
    groups, together = outs[0].shape[1], held.shape[0] // outs[0].shape[1]
    functions = src.shape[1]
    tiles, high = LANES // 128, GRID_N // XG

    def fetch(group):
        part = pl.ds(together * group, together)
        return pltpu.make_async_copy(src.at[part], held.at[part], arrived.at[group])

    for group in range(groups):
        fetch(group).start()
    for group in range(groups):
        fetch(group).wait()
        for x in range(together):
            for y in range(high):
                for t in range(tiles):
                    cut = slice(y * LANES + 128 * t, y * LANES + 128 * t + 128)
                    rows[x * tiles + t, y * functions:(y + 1) * functions, :] = held[together * group + x, :, cut].astype(F32)
        for first, out in zip(firsts, outs, strict=True):
            for f in range(out.shape[0]):
                at = pl.ds(first(blocks) + f, high, stride=functions)
                wide = [jnp.concatenate([rows[x * tiles + t, at, :] for t in range(tiles)], axis=1) for x in range(together)]
                wide += [jnp.zeros((high, LANES), F32)] * (XG - together)
                lines = [
                    jnp.concatenate([w[:, GRID_N * low:GRID_N * low + GRID_N] for w in wide], axis=1) for low in range(XG)
                ]
                out[f, group] = jnp.concatenate(lines, axis=0).astype(BF16)


def planes(orbitals, blocks, firsts, count, stay=False):
    orbitals = jnp.transpose(orbitals, (1, 0, 2))
    slab, functions, size = orbitals.shape
    together = min(XG, slab)
    groups = slab // together
    shape = (count, groups, GRID_N, LANES)
    spec = pltpu.PrefetchScalarGridSpec(
        num_scalar_prefetch=1,
        grid=(1,),
        in_specs=[pl.BlockSpec(memory_space=pl.ANY)],
        out_specs=[pl.BlockSpec(shape, lambda g, b: (0, 0, 0, 0))] * len(firsts),
        scratch_shapes=[
            pltpu.VMEM((LANES // 128 * together, (GRID_N // XG + 1) * functions, 128), F32),
            pltpu.VMEM((slab, functions, size), BF16),
            pltpu.SemaphoreType.DMA((groups,)),
        ],
    )
    return pl.pallas_call(
        functools.partial(planes_kernel, firsts),
        grid_spec=spec,
        out_shape=[jax.ShapeDtypeStruct(shape, BF16)] * len(firsts),
        compiler_params=pltpu.CompilerParams(vmem_limit_bytes=WHOLE_VMEM if stay else PART_VMEM),
        cost_estimate=pl.CostEstimate(flops=0, bytes_accessed=4 * slab * functions * size, transcendentals=0),
        name="planes",
    )(blocks, orbitals)


def tables_kernel(*refs):
    *points, phases, pick, wave = refs
    cols = pick.shape[1]
    phase = phases[lax.axis_index("grid")]
    for r in range(pick.shape[0]):
        half = points[0].shape[0]
        point = points[r // half][r % half:r % half + 1, :]
        shape = (cols, point.shape[1])
        found = lax.broadcasted_iota(jnp.int32, shape, 0) == jnp.broadcast_to(point & (cols - 1), shape)
        pick[r] = found.astype(F32).astype(BF16)
        shape = (KF, point.shape[1])
        turn = lax.broadcasted_iota(jnp.int32, shape, 0) == jnp.broadcast_to(point >> (cols.bit_length() - 1), shape)
        turn = turn.astype(F32).astype(BF16)
        wave[r] = sum(jnp.dot(phase[i], turn, preferred_element_type=F32) for i in range(2))


def tables(points, phases, cols):
    targets, own = 2 * points[0].shape[0], points[0].shape[1]
    return pl.pallas_call(
        tables_kernel,
        out_shape=[
            jax.ShapeDtypeStruct((targets, cols, own), BF16),
            jax.ShapeDtypeStruct((targets, phases.shape[2], own), F32),
        ],
        compiler_params=pltpu.CompilerParams(vmem_limit_bytes=16 * 1024 * 1024),
        cost_estimate=pl.CostEstimate(flops=0, bytes_accessed=3 * targets * cols * own, transcendentals=0),
        name="tables",
    )(*points, phases)


def front_kernel(sources, find, blocks, source_of, *refs):
    parts_in, refs = refs[:sources], refs[sources:]
    cond, ytab, ztab, pick, wave, even, odd, vals, mixed, section, arrived = refs
    conds, groups = cond.shape[0], cond.shape[1]
    cols = pick.shape[1]
    own_y = cols // KF
    classes = ztab.shape[0]
    each = KF // classes
    count = vals.shape[0]
    for f in range(count):
        wanted, inside = find(blocks, source_of, f)
        for s in range(sources):
            @pl.when(wanted == s)
            def _(f=f, s=s):
                pltpu.make_async_copy(parts_in[s].at[inside], vals.at[f], arrived.at[f]).start()

    units = [(pair, group) for pair in range(conds // 2) for group in range(groups)]
    rows = 2 * each

    def sections(now, carry):
        pltpu.make_async_copy(parts_in[0].at[0], vals.at[now], arrived.at[now]).wait()
        for first in range(0, len(units), 2):
            two = units[first:first + 2]
            density = [
                jnp.concatenate([vals[now, group] * cond[2 * pair + i, group] for pair, group in two], axis=1) for i in range(2)
            ]
            out = jnp.dot(ytab[...], jnp.concatenate(density, axis=0), preferred_element_type=F32).astype(BF16)
            for i, (pair, group) in enumerate(two):
                at = (group * conds + 2 * pair) * each
                for kind in range(classes):
                    for half in range(2):
                        base = (half * classes + kind) * rows
                        mixed[kind, at:at + rows, half * LANES:half * LANES + LANES] = out[base:base + rows, i * LANES:i * LANES + LANES]
        for kind in range(classes):
            value = jnp.dot(mixed[kind], ztab[kind], preferred_element_type=F32)
            section[now, 2 * kind, :value.shape[0], :] = value[:, :128]
            section[now, 2 * kind + 1, :value.shape[0], :] = value[:, 128:]
        return carry

    lax.fori_loop(0, count, sections, 0)
    place = lax.broadcasted_iota(jnp.int32, (conds, 128), 1) // KF
    planes_in = [(group, half) for group in range(groups) for half in range(2)]

    def rows_of(f, kind, half, group, k):
        return section[f, 2 * kind + half, pl.ds(group * conds * each + k, conds, stride=each), :]

    def pieces_of(f, target):
        if classes == 1:
            parts = []
            for group, half in planes_in:
                rows = [rows_of(f, 0, half, group, target * own_y + y) for y in range(own_y)]
                for piece in range(4):
                    cut = slice(KF * piece, KF * piece + KF)
                    parts.append(jnp.concatenate([row[:, cut] for row in rows], axis=1))
            return parts
        found = {}
        loaded = [[rows_of(f, kind, half, group, target) for kind in range(classes)] for group, half in planes_in]
        for piece in range(4):
            merged = []
            for rows in loaded:
                value = rows[-piece % 4]
                for slot in range(1, 4):
                    value = jnp.where(place == slot, rows[(slot - piece) % 4], value)
                merged.append(value)
            turned = jnp.concatenate(merged, axis=0)
            if piece:
                turned = pltpu.roll(turned, 128 - KF * piece, 1)
            for i in range(len(planes_in)):
                found[4 * i + piece] = turned[i * conds:(i + 1) * conds]
        return [found[i] for i in range(4 * len(planes_in))]

    def folded(f, target):
        parts = pieces_of(f, target)
        planes_count = len(parts) // 2
        out = []
        for x in range(planes_count // 2):
            high = planes_count - 1 - x
            out += [parts[2 * high + i] + parts[2 * x + i] for i in range(2)]
            out += [parts[2 * high + i] - parts[2 * x + i] for i in range(2)]
        return out

    def one_target(step, parity, out_ref):
        order = target_of(step, pick.shape[0]) + parity
        target = lax.axis_index("grid").astype(jnp.int32) ^ order
        parts = [folded(f, target) for f in range(count)]
        lines = XG * groups // 2
        left = jnp.concatenate([p for part in parts for p in part], axis=0).astype(BF16)
        found = jnp.dot(left, pick[order], preferred_element_type=F32)
        turn = [wave[order, i:i + 1, :] for i in range(2 * lines + 2)]
        for f in range(count):
            real = imag = None
            for x in range(lines):
                cosine, sine = turn[x], turn[lines + x]
                base = 4 * (f * lines + x) * conds
                sum_re, sum_im, diff_re, diff_im = (found[base + i * conds:base + (i + 1) * conds] for i in range(4))
                add_real = sum_re * cosine + diff_im * sine
                add_imag = sum_im * cosine - diff_re * sine
                real = add_real if real is None else real + add_real
                imag = add_imag if imag is None else imag + add_imag
            cosine, sine = turn[2 * lines], turn[2 * lines + 1]
            both = [real * cosine + imag * sine, imag * cosine - real * sine]
            out_ref[step, 2 * conds * f:2 * conds * f + 2 * conds, :] = jnp.concatenate(both, axis=0).astype(BF16)

    def body(step, carry):
        one_target(step, 0, even)
        one_target(step, 1, odd)
        return carry

    lax.fori_loop(0, even.shape[0], body, 0)


def front(find, count, blocks, sources, cond, ytab, ztab, pick, wave):
    conds, groups = cond.shape[:2]
    targets, cols, own = pick.shape
    classes = ztab.shape[0]
    rows = 2 * conds
    shape = jax.ShapeDtypeStruct((targets // 2, count * rows, own), BF16)
    inside, scalars = pl.BlockSpec(memory_space=pltpu.VMEM), pl.BlockSpec(memory_space=pltpu.SMEM)
    return pl.pallas_call(
        functools.partial(front_kernel, len(sources), find),
        in_specs=[scalars] * 2 + [pl.BlockSpec(memory_space=pl.ANY)] * len(sources) + [inside] * 5,
        out_specs=[inside] * 2,
        scratch_shapes=[
            pltpu.VMEM((count,) + cond.shape[1:], BF16),
            pltpu.VMEM((classes, groups * conds * KF // classes, 2 * LANES), BF16),
            pltpu.VMEM((count, 2 * classes, (groups * conds + 1) * KF // classes, XG * KF), F32),
            pltpu.SemaphoreType.DMA((count,)),
        ],
        out_shape=[shape, shape],
        compiler_params=pltpu.CompilerParams(vmem_limit_bytes=FRONT_VMEM),
        cost_estimate=pl.CostEstimate(flops=count * 900_000_000, bytes_accessed=count * 2_000_000, transcendentals=0),
        name="front",
    )(blocks, jnp.asarray(SOURCES.reshape(-1), jnp.int32), *sources, cond, ytab, ztab, pick, wave)


def screen_kernel(split, parity, *refs):
    *pieces, screened, out = refs
    sums = []
    for i, count in enumerate(split):
        group = pieces[sum(split[:i]):sum(split[:i]) + count]
        total = group[0][...].astype(F32)
        for piece in group[1:]:
            total = total + piece[...].astype(F32)
        sums.append(total.astype(BF16))
    side = jnp.concatenate(sums, axis=0)
    steps, _, own = out.shape
    here = lax.axis_index("grid").astype(jnp.int32)

    def step(r, carry):
        target = here ^ target_of(r, 2 * steps) ^ parity
        columns = screened[:, pl.ds(pl.multiple_of(target * own, own), own)]
        out[r] = jnp.dot(side, columns, preferred_element_type=F32).astype(BF16)
        return carry

    lax.fori_loop(0, steps, step, 0)


def screen(parts, screened, targets, parity):
    own = parts[0][0].shape[1]
    rows = sum(p[0].shape[0] for p in parts)
    flat = [piece for part in parts for piece in part]
    if own % 128:
        here = lax.axis_index("grid").astype(jnp.int32)
        side = jnp.concatenate([sum(p.astype(F32) for p in part) for part in parts], axis=0).astype(BF16)
        part = jnp.dot(side, screened, preferred_element_type=F32).astype(BF16)
        part = jnp.transpose(part.reshape(rows, targets, own), (1, 0, 2))
        wanted = here ^ target_of(jnp.arange(targets // 2, dtype=jnp.int32), targets) ^ parity
        return jnp.take(part, wanted, axis=0)
    inside = pl.BlockSpec(memory_space=pltpu.VMEM)
    return pl.pallas_call(
        functools.partial(screen_kernel, [len(p) for p in parts], parity),
        in_specs=[inside] * (len(flat) + 1),
        out_specs=inside,
        out_shape=jax.ShapeDtypeStruct((targets // 2, rows, own), BF16),
        compiler_params=pltpu.CompilerParams(vmem_limit_bytes=PART_VMEM),
        cost_estimate=pl.CostEstimate(flops=rows * own * own * targets, bytes_accessed=own * own * targets, transcendentals=0),
        name="screen",
    )(*flat, screened)


def close_kernel(split, place, blocks, slot_of, *refs):
    ins, outs, sums = refs[:sum(map(sum, split))], refs[sum(map(sum, split)):-2], refs[-2:]
    chunks, functions, unit, _ = sums[0].shape
    half = unit // 2
    for side, pieces in enumerate(split):
        first = 0
        for count in pieces:
            group, ins = ins[:count], ins[count:]
            here = group[0].shape[1] // unit
            for chunk in range(chunks):
                total = group[0][chunk].astype(F32)
                for piece in group[1:]:
                    total = total + piece[chunk].astype(F32)
                sums[side][chunk, first:first + here] = total.reshape(here, unit, total.shape[1])
            first += here
    slots = [[place(blocks, slot_of, side, f) for f in range(functions)] for side in range(2)]
    product = None
    for chunk in range(chunks):
        for part in range(2):
            rows = slice(half * part, half * part + half)
            left, right = (
                jnp.concatenate([sums[side][chunk, slot][rows] for slot in slots[side]], axis=0).astype(BF16) for side in range(2)
            )
            term = lax.dot_general(left, right, (((1,), (1,)), ((), ())), preferred_element_type=F32)
            product = term if product is None else product + term
    if len(outs) == 1:
        outs[0][...] = product
    else:
        steps, rows = outs[0].shape[:2]
        for step in range(steps):
            for parity in range(2):
                first = (target_of(step, 2 * steps) + parity) * rows
                outs[parity][step] = product[first:first + rows]


def close(place, blocks, u_parts, b_parts, conds, targets, by_target):
    split = [[len(p) for p in side] for side in (u_parts, b_parts)]
    flat = [x for side in (u_parts, b_parts) for p in side for x in p]
    functions = BLK
    rows = functions * conds
    chunks, _, own = flat[0].shape
    if by_target:
        out = [jax.ShapeDtypeStruct((targets // 2, rows // targets, rows), F32)] * 2
    else:
        out = [jax.ShapeDtypeStruct((rows, rows), F32)]
    spec = pltpu.PrefetchScalarGridSpec(
        num_scalar_prefetch=2,
        grid=(1,),
        in_specs=[pl.BlockSpec(x.shape, lambda i, b, t: (0, 0, 0)) for x in flat],
        out_specs=[pl.BlockSpec(o.shape, lambda i, b, t, o=o: (0,) * len(o.shape)) for o in out],
        scratch_shapes=[pltpu.VMEM((chunks, functions, 2 * conds, own), F32)] * 2,
    )
    return pl.pallas_call(
        functools.partial(close_kernel, split, place),
        grid_spec=spec,
        out_shape=out,
        cost_estimate=pl.CostEstimate(flops=4 * rows * rows * own, bytes_accessed=8 * rows * own, transcendentals=0),
        compiler_params=pltpu.CompilerParams(vmem_limit_bytes=24 * 1024 * 1024),
        name="close",
    )(blocks, jnp.asarray(slots_of().reshape(-1), jnp.int32), *flat)


def swap(array, axis, mask, size):
    return lax.ppermute(array, axis, [(i, i ^ mask) for i in range(size)])


def target_of(step, targets):
    bits = (targets // 2).bit_length() - 1
    return 2 * sum(((step >> i) & 1) << (bits - 1 - i) for i in range(bits))


def after(value, *others):
    return lax.optimization_barrier((value, *others))[0]


def add(left, right):
    return (left.astype(F32) + right.astype(F32)).astype(left.dtype)


def halve(kept, got, mask, targets):
    half = kept.shape[0] // 2
    sent = add(kept[half:], got[half:])
    return add(kept[:half], got[:half]), swap(sent, "grid", mask, targets), sent


def halving(even, odd, targets):
    got = swap(odd, "grid", 1, targets)
    mask = 2
    while even.shape[0] > 1:
        even, got, _ = halve(even, got, mask, targets)
        mask *= 2
    return [even[0], got[0]]


def both_blocks(kept, got, targets):
    total = add(kept, got)
    come = swap(total, "grid", targets // 2, targets)
    return [total, come[::-1]]


def round_ring(own, holder, size, reverse):
    order = list(range(size))
    if reverse:
        order = order[::-1]
    pairs = [(order[i], order[(i + 1) % size]) for i in range(size)]
    place = [0] * size
    for i, device in enumerate(order):
        place[device] = i
    place = jnp.array(place, jnp.int32)
    away = (place[lax.axis_index("band")] - place[holder]) % size
    chunks = len(own)
    got = []
    for step in range(chunks + size - 2):
        mine = own[min(step, chunks - 1)]
        sent = mine if step == 0 else jnp.where(away == 0, mine, got[-1])
        got.append(lax.ppermute(sent, "band", pairs))
    out = []
    for j in range(chunks):
        value = own[j]
        for hop in range(1, size):
            value = jnp.where(away == hop, got[j + hop - 1], value)
        out.append(value)
    return out


def by_ring(valence, blocks, side, held, size):
    half = BLK // 2
    own = planes(valence, blocks, [lambda b, j=j: b[side] % held * BLK + j for j in range(BLK)], 1)
    right = round_ring(own[:half], blocks[side] // held, size, False)
    left = round_ring(own[half:], blocks[side] // held, size, True)
    return right, left


class Swaps:
    def __init__(self, own, owner):
        self.own, self.owner = own, owner
        self.got = [(own[0], own[1])]
        self.sent = [(own[0], own[1])]

    def send(self):
        across, along = self.sent[-1]
        self.got.append((swap(across, "band", 1, 4), swap(along, "band", 2, 4)))

    def choose(self):
        x, y = self.got[-1]
        ahead = (2, 3) if len(self.got) == 2 else (3, 2)
        self.sent.append(tuple(jnp.where(self.owner, self.own[q], a) for q, a in zip(ahead, (y, x), strict=True)))

    def sources(self, late):
        if late:
            return [*self.own[2:], *self.got[3]]
        return [*self.own[:2], *self.got[1], *self.got[2]]


def per_device(sizes, valence, conduction, screened, blocks, gsphere):
    n_band, n_grid = sizes
    held = valence.shape[0] // BLK
    conds, own = conduction.shape[0], gsphere.shape[0]
    cols = KF // n_grid * KF
    half, quarter = BLK // 2, BLK // 4
    swaps = n_band == 4
    at = lax.axis_index("grid").astype(jnp.int32)[None]
    cosine, sine = fourier_parts(GRID_N, KF)
    classes = classes_of(cols // KF)
    ytab, ztab = (jnp.asarray(t(cosine, sine, classes)) for t in (y_table, z_table))

    def role(b, side):
        return lax.axis_index("band").astype(jnp.int32) ^ (b[side] // held)

    def quarters(wanted, stay=False):
        firsts = [lambda b, s=s, q=q: b[s] % held * BLK + quarter * q for s, q in wanted]
        return planes(valence, blocks, firsts, quarter, stay)

    def more(points, i):
        return jnp.concatenate([points, swap(points, "grid", 1 << i, n_grid)], axis=0)

    points = gsphere.reshape(1, own)
    levels = n_grid.bit_length() - 1
    if swaps:
        own_a = quarters([(0, 0), (0, 1)], True)
        own_b = quarters([(1, 0), (1, 1), (0, 2), (0, 3), (1, 2), (1, 3)])
        a, b = (
            Swaps(o, lax.axis_index("band") == blocks[s] // held)
            for s, o in enumerate(([*own_a, *own_b[2:4]], [*own_b[:2], *own_b[4:]]))
        )
        a.send()
        a.choose()
        a.send()
        b.send()
        a.choose()
        a.send()
        points = after(points, *a.sent[1])
        conduction = after(conduction, *a.sent[1])
        for i in range(levels - 1):
            points = more(points, i)
        last = swap(points, "grid", n_grid // 2, n_grid)
        sources = lambda side, late: (a, b)[side].sources(late)
    else:
        rings = [by_ring(valence, blocks, s, held, n_band) for s in range(2)]
        sources = lambda side, late: rings[side][late]
        for i in range(levels - 1):
            points = more(points, i)
        last = swap(points, "grid", n_grid // 2, n_grid)
    cond, = planes(conduction, blocks, [lambda b: 0], conds)
    pick, wave = tables([points, last], jnp.asarray(x_phases(n_grid)), cols)

    def part(side, late, *others):
        def find(b, source_of, f):
            if not swaps:
                return f, 0
            return source_of[role(b, side) * 4 + 2 * late + f // quarter], f % quarter
        return front(find, half, after(blocks, *others), sources(side, late), cond, ytab, ztab, pick, wave)

    def core(pair):
        return pair[0], swap(pair[1], "grid", 1, n_grid)

    early_a = core(part(0, 0, *(a.sent[2] if swaps else ())))
    if swaps:
        b.got[1] = lax.optimization_barrier((*b.got[1], early_a[0]))[:2]
        b.choose()
        b.send()
    early_a = halve(*early_a, 2, n_grid)
    late_a = core(part(0, 1, early_a[2]))
    late_a = halve(*late_a, 2, n_grid)
    if swaps:
        b.choose()
        b.send()
    early_b = core(part(1, 0, late_a[2], *(b.sent[2] if swaps else ())))
    side_a = [after(early_a[0], early_b[0]), early_a[1]], [late_a[0], late_a[1]]
    side_a = [jnp.concatenate([e, l], axis=1) for e, l in zip(*side_a, strict=True)]
    side_a = halve(*side_a, 4, n_grid)
    early_b = halve(*early_b, 2, n_grid)
    late_b = core(part(1, 1, side_a[2], early_b[2]))

    def finish(pair, mask):
        pair = pair[:2]
        while pair[0].shape[0] > 1:
            pair = halve(*pair, mask, n_grid)[:2]
            mask *= 2
        return [p[0] for p in pair]

    def until_two(pair, mask):
        pair = pair[:2]
        while pair[0].shape[0] > 2:
            pair = halve(*pair, mask, n_grid)[:2]
            mask *= 2
        return pair

    side_a = [finish(side_a, 8)]
    early_b = both_blocks(*until_two(early_b, 4), n_grid)
    odd_u = screen([[after(side_a[0][0], late_b[0], early_b[0]), *side_a[0][1:]]], screened, n_grid, 1)
    late_b = halve(*late_b, 2, n_grid)
    even_u = screen([[after(side_a[0][0], odd_u, late_b[2]), *side_a[0][1:]]], screened, n_grid, 0)
    part_u = until_two(core((even_u, odd_u)), 2)
    side_b = [early_b, both_blocks(*until_two(late_b, 4), n_grid)]

    by_target = n_grid == BLK

    def place(b, slot_of, side, f):
        if side == 0 and by_target:
            f = f ^ lax.axis_index("grid").astype(jnp.int32)
        return slot_of[role(b, side) * BLK + f] if swaps else f

    shares = close(place, blocks, [part_u], side_b, conds, n_grid, by_target)
    if not by_target:
        share = shares[0].reshape(n_grid, -1, shares[0].shape[1])
        even = at ^ target_of(jnp.arange(n_grid // 2, dtype=jnp.int32), n_grid)
        shares = jnp.take(share, even, axis=0), jnp.take(share, even ^ 1, axis=0)
    share = add(shares[0], swap(shares[1], "grid", 1, n_grid))
    far = [swap(share[i], "grid", target_of(i, n_grid), n_grid) for i in range(1, n_grid // 2)]
    return sum(far, share[0])[None]


def solution(mesh):
    sizes = (mesh.shape["band"], mesh.shape["grid"])
    in_specs = (P("band", "grid", None), P("band", "grid", None), P("grid", None), P(), P("grid"))
    out_specs = P("band", "grid", None)
    return jax.shard_map(
        functools.partial(per_device, sizes), mesh=mesh, in_specs=in_specs, out_specs=out_specs, check_vma=False
    )
```
